32 devices in a mesh: group: 2 (over x), row: 16 (over z, y, core).
Axes of the slice: x: 2, y: 2, z: 4, core: 2. Of those that a mesh axis runs over, the one named last changes fastest.
Arguments:
- fine_features: bfloat16 [256, 256, 192], P(None, ('group', 'row')), parts along dimension 1, may hold values from -6 to 6
- section_two: bfloat16 [128, 128, 384], P('row', 'group'), parts along dimension 1, may hold values from -6 to 6
- section_three: bfloat16 [64, 64, 768], P('row', 'group'), parts along dimension 1, may hold values from -6 to 6
- section_four: bfloat16 [32, 32, 1536], P('row', 'group'), parts along dimension 1, may hold values from -6 to 6
- strip_map: int32 [32], P('group'), parts along dimension 0, may hold values from 0 to 15, each once
- lateral_one: bfloat16 [192, 512], replicated, may hold values from -0.4375 to 0.4375
- lateral_two: bfloat16 [384, 512], replicated, may hold values from -0.3125 to 0.3125
- lateral_three: bfloat16 [768, 512], replicated, may hold values from -0.21875 to 0.21875
- lateral_four: bfloat16 [1536, 512], replicated, may hold values from -0.15625 to 0.15625
- join_weight: bfloat16 [512, 512], replicated, may hold values from -0.25 to 0.25
- cotangent: bfloat16 [256, 256, 512], P(None, ('group', 'row')), parts along dimension 1, may hold values from -6 to 6
Outputs:
- grad_fine: bfloat16 [256, 256, 192], P(None, ('group', 'row')), parts along dimension 1
- grad_two: bfloat16 [128, 128, 384], P('row', 'group'), parts along dimension 1
- grad_three: bfloat16 [64, 64, 768], P('row', 'group'), parts along dimension 1
- grad_four: bfloat16 [32, 32, 1536], P('row', 'group'), parts along dimension 1
- grad_join: float32 [1024, 512], P('group', 'row'), parts along dimension 0
- grad_lateral_one: float32 [384, 512], P(('group', 'row')), parts along dimension 0
- grad_lateral_two: float32 [768, 512], P(('group', 'row')), parts along dimension 0
- grad_lateral_three: float32 [1536, 512], P(('group', 'row')), parts along dimension 0
- grad_lateral_four: float32 [3072, 512], P(('group', 'row')), parts along dimension 0
The draws below stay inside these ranges and needn't reach their ends.
There are 2 independent parts, one for each index of `group`. The reference program is written for one: setup_inputs(seed, part) draws one part's arguments, and reference() takes and returns one part's arrays. A program takes and returns all parts, laid end to end along the dimension named above; an argument that names none is the same for every part. Nothing has to cross between parts.
Inputs may be any that keep to these rules, and one draw needn't show every extreme that they name: strip_map holds each strip number of 0 to 15 once.
All inputs are finite; a program needn't handle non-finite values.
Results may differ from the reference program's by a relative error of at most 0.01.
Values may be sent and summed in bfloat16 or wider, within the bound.
No kernel may reach another device: no remote copies, remote signals or barrier semaphores. Data moves between devices by JAX's collectives and lax.ppermute only.
A program may use at most 128 MiB of HBM per device.

```python
import jax
import jax.numpy as jnp
from jax import lax

C1 = 192
C2 = 384
C3 = 768
C4 = 1536
F = 512
FH = 256
FWD = 8
FW = 128
N_ROW = 16


def raised(result, key, source, target, blocks, factor):
    def block_of(position):
        return (jnp.arange(result.shape[position]) // (result.shape[position] // blocks)).reshape((-1,) + (1,) * (result.ndim - 1 - position))

    near = jax.random.permutation(key, blocks)[block_of(target)]
    other_side = (block_of(target) + blocks // 2) % blocks
    return jnp.where((block_of(source) == near) | (block_of(source) == other_side), factor * result, result)


def steps_of(key, shape, cuts, smallest, top_value):
    def one(dim, parts):
        steps = jax.random.uniform(jax.random.fold_in(jax.random.fold_in(key, 6), dim), (parts,), jnp.float32, smallest / len(cuts), top_value / len(cuts))
        return jnp.repeat(jnp.exp(steps), shape[dim] // parts).reshape((-1,) + (1,) * (len(shape) - dim - 1))

    factor_of = one(*cuts[0])
    for cut in cuts[1:]:
        factor_of = factor_of * one(*cut)
    return factor_of


def centred(own_key, shape, scale, reach, cuts=(), held_as=jnp.bfloat16):
    loudness = steps_of(own_key, shape, cuts, -0.22, 0.18) if cuts else 1.0
    drawn = jax.random.normal(own_key, shape, jnp.float32) * scale * loudness
    return jnp.minimum(jnp.maximum(drawn, -reach), reach).astype(held_as)


def bell_draw_with(stream_key, dims, width, reach, cuts, heavy, kind=jnp.bfloat16):
    values = width * jax.random.normal(stream_key, dims, jnp.float32)
    if cuts:
        values = values * steps_of(stream_key, dims, cuts, -0.22, 0.18)
    return jnp.clip(raised(values, jax.random.fold_in(stream_key, 3), *heavy), -reach, reach).astype(kind)


def setup_inputs(seed: int = 0, part: int = 0) -> dict:
    key_of = jax.random.split(jax.random.key(seed), 12)
    own_keys = jax.random.split(jax.random.fold_in(key_of[11], part), 12)
    return {
        "fine_features": bell_draw_with(own_keys[0], (FH, FW, C1), 1.0, 6.0, ((1, 16),), (1, 2, 16, 2.0)),
        "section_two": bell_draw_with(own_keys[1], (FH // 2, FW // 2, C2), 1.0, 6.0, ((0, 16),), (0, 2, 16, 2.0)),
        "section_three": bell_draw_with(own_keys[2], (FH // 4, FW // 4, C3), 1.0, 6.0, ((0, 16),), (0, 2, 16, 2.0)),
        "section_four": bell_draw_with(own_keys[3], (FH // 8, FW // 8, C4), 1.0, 6.0, ((0, 16),), (0, 2, 16, 2.0)),
        "strip_map": jax.random.permutation(own_keys[4], N_ROW).astype(jnp.int32),
        "lateral_one": centred(key_of[5], (C1, F), C1 ** -0.5, 0.4375),
        "lateral_two": centred(key_of[6], (C2, F), C2 ** -0.5, 0.3125),
        "lateral_three": centred(key_of[7], (C3, F), C3 ** -0.5, 0.21875),
        "lateral_four": centred(key_of[8], (C4, F), C4 ** -0.5, 0.15625),
        "join_weight": centred(key_of[9], (F, F), F ** -0.5, 0.25),
        "cotangent": bell_draw_with(own_keys[10], (FH, FW, F), 1.0, 6.0, ((1, 16),), (1, 2, 16, 2.0)),
    }


def phase_weights(phase_index, factor):
    offset = (phase_index + 0.5) / factor - 0.5
    if offset < 0:
        return 0, -offset, 1.0 + offset
    return 1, 1.0 - offset, offset


def edge_pad(values, dimension):
    length = values.shape[dimension]
    head_row = lax.slice_in_dim(values, 0, 1, axis=dimension)
    tail_row = lax.slice_in_dim(values, length - 1, length, axis=dimension)
    return jnp.concatenate([head_row, values, tail_row], axis=dimension)


def fold_edges(padded, dimension):
    length = padded.shape[dimension] - 2
    head_row = lax.slice_in_dim(padded, 0, 1, axis=dimension) + lax.slice_in_dim(padded, 1, 2, axis=dimension)
    middle = lax.slice_in_dim(padded, 2, length, axis=dimension)
    tail_row = lax.slice_in_dim(padded, length, length + 1, axis=dimension) + lax.slice_in_dim(padded, length + 1, length + 2, axis=dimension)
    return jnp.concatenate([head_row, middle, tail_row], axis=dimension)


def upsample_padded(padded, factor, dimension):
    length = padded.shape[dimension] - 2
    phases = []
    for phase_index in range(factor):
        start_index, lower_weight, upper_weight = phase_weights(phase_index, factor)
        lower_part = lax.slice_in_dim(padded, start_index, start_index + length, axis=dimension)
        upper_part = lax.slice_in_dim(padded, start_index + 1, start_index + 1 + length, axis=dimension)
        phases.append(lower_weight * lower_part + upper_weight * upper_part)
    stacked = jnp.stack(phases, axis=dimension + 1)
    new_shape = list(padded.shape)
    new_shape[dimension] = length * factor
    return stacked.reshape(tuple(new_shape))


def adjoint_padded(gradient, factor, dimension):
    length = gradient.shape[dimension] // factor
    split_shape = gradient.shape[:dimension] + (length, factor) + gradient.shape[dimension + 1:]
    split_grad = gradient.reshape(split_shape)
    summed = None
    for phase_index in range(factor):
        start_index, lower_weight, upper_weight = phase_weights(phase_index, factor)
        phase_part = lax.index_in_dim(split_grad, phase_index, axis=dimension + 1, keepdims=False)
        lower_pad = [(0, 0)] * gradient.ndim
        lower_pad[dimension] = (start_index, 2 - start_index)
        upper_pad = [(0, 0)] * gradient.ndim
        upper_pad[dimension] = (start_index + 1, 1 - start_index)
        phase_term = jnp.pad(lower_weight * phase_part, lower_pad) + jnp.pad(upper_weight * phase_part, upper_pad)
        summed = phase_term if summed is None else summed + phase_term
    return summed


def extend_blocks(values, pieces):
    row_count, column_count, channels = values.shape
    block_width = column_count // pieces
    padded = edge_pad(values, 1)
    main_cols = values.reshape(row_count, pieces, block_width, channels)
    left_cols = lax.slice_in_dim(padded, 0, column_count, stride=block_width, axis=1)
    right_cols = lax.slice_in_dim(padded, block_width + 1, column_count + 2, stride=block_width, axis=1)
    return jnp.concatenate([left_cols[:, :, None], main_cols, right_cols[:, :, None]], axis=2)


def fold_blocks(blocks):
    row_count, pieces, extended, channels = blocks.shape
    block_width = extended - 2
    column_count = pieces * block_width
    main_cols = blocks[:, :, 1:block_width + 1].reshape(row_count, column_count, channels)
    zero_fill = jnp.zeros((row_count, pieces, block_width - 1, channels), blocks.dtype)
    left_cols = jnp.concatenate([blocks[:, :, 0:1], zero_fill], axis=2).reshape(row_count, column_count, channels)
    right_cols = jnp.concatenate([zero_fill, blocks[:, :, block_width + 1:]], axis=2).reshape(row_count, column_count, channels)
    padded = jnp.pad(main_cols, ((0, 0), (1, 1), (0, 0))) + jnp.pad(left_cols, ((0, 0), (0, 2), (0, 0))) + jnp.pad(right_cols, ((0, 0), (2, 0), (0, 0)))
    return fold_edges(padded, 1)


def project_rows(values, weight):
    flat = values.reshape(-1, values.shape[-1])
    product = jnp.dot(flat, weight, preferred_element_type=jnp.float32).astype(jnp.bfloat16)
    return product.reshape(values.shape[:-1] + (weight.shape[1],))


def contract_rows(left_rows, right_rows):
    return lax.dot_general(left_rows, right_rows, (((0,), (0,)), ((), ())), preferred_element_type=jnp.float32)


def inverse_map(strip_map, pieces):
    positions = jnp.arange(pieces, dtype=jnp.int32)
    matches = (strip_map.astype(jnp.int32)[None, :] == positions[:, None]).astype(jnp.int32)
    return jnp.sum(matches * positions[None, :], axis=1).astype(jnp.int32)


def upsample_map(lateral_ext, factor, row_dim, column_dim):
    vertical = upsample_padded(edge_pad(lateral_ext.astype(jnp.float32), row_dim), factor, row_dim)
    return upsample_padded(vertical, factor, column_dim)


def adjoint_map(gradient, factor, row_dim, column_dim):
    across = adjoint_padded(gradient, factor, column_dim)
    down = fold_edges(adjoint_padded(across, factor, row_dim), row_dim)
    return down.astype(jnp.bfloat16)


def reference(fine_features, section_two, section_three, section_four, strip_map, lateral_one, lateral_two, lateral_three, lateral_four, join_weight, cotangent):
    pieces = N_ROW
    strip_index = strip_map.astype(jnp.int32)
    inverse = inverse_map(strip_index, pieces)
    sections = ((section_two, lateral_two, 2), (section_three, lateral_three, 4), (section_four, lateral_four, 8))
    fine_flat = fine_features.reshape(-1, C1)
    joined = jnp.dot(fine_flat, lateral_one, preferred_element_type=jnp.float32).reshape(FH, pieces, FWD, F)
    for features, weight, factor in sections:
        extended = extend_blocks(project_rows(features, weight), pieces)
        upsampled = upsample_map(extended, factor, 0, 2)
        joined = joined + jnp.take(upsampled, strip_index, axis=1)
    sigmoid_part = jax.nn.sigmoid(joined)
    hidden = (joined * sigmoid_part).astype(jnp.bfloat16)
    hidden_flat = hidden.reshape(-1, F)
    cotangent_flat = cotangent.reshape(-1, F)
    grad_join = contract_rows(hidden_flat, cotangent_flat)
    hidden_grad = jnp.dot(cotangent_flat, join_weight.T, preferred_element_type=jnp.float32)
    slope = sigmoid_part * (1.0 + joined * (1.0 - sigmoid_part))
    joined_grad = (hidden_grad * slope.reshape(-1, F)).astype(jnp.bfloat16)
    grad_fine = jnp.dot(joined_grad, lateral_one.T, preferred_element_type=jnp.float32).astype(jnp.bfloat16).reshape(fine_features.shape)
    grad_lateral_one = contract_rows(fine_flat, joined_grad)
    strip_grad = jnp.take(joined_grad.reshape(FH, pieces, FWD, F), inverse, axis=1).astype(jnp.float32)
    results = []
    for features, weight, factor in sections:
        lateral_grad = adjoint_map(strip_grad, factor, 0, 2)
        flat_grad = lateral_grad.reshape(-1, F)
        channels = weight.shape[0]
        feature_grad = jnp.dot(flat_grad, weight.T, preferred_element_type=jnp.float32).reshape(lateral_grad.shape[:3] + (channels,))
        grad_section = fold_blocks(feature_grad).astype(jnp.bfloat16)
        extended = extend_blocks(features, pieces).reshape(-1, channels)
        results.append((grad_section, contract_rows(extended, flat_grad)))
    return (grad_fine, results[0][0], results[1][0], results[2][0], grad_join, grad_lateral_one, results[0][1], results[1][1], results[2][1])
```

```python
import functools

import jax
import jax.numpy as jnp
import numpy as np
from jax import lax
from jax.experimental import pallas as pl
from jax.experimental.pallas import tpu as pltpu
from jax.sharding import PartitionSpec as P

F32 = jnp.float32
BF16 = jnp.bfloat16
FACTORS = (2, 4, 8)
LANES = 128
VMEM = pl.BlockSpec(memory_space=pltpu.VMEM)
SMEM = pl.BlockSpec(memory_space=pltpu.SMEM)
MEBI = 1024 * 1024


def round_up(value, multiple):
    return -(-value // multiple) * multiple


class Plan:
    def __init__(self, owners, depth, strip_width, channels, width):
        self.owners, self.depth, self.strip_width = owners, depth, strip_width
        self.width = width
        self.rows = [depth * 8 // k for k in FACTORS]
        self.columns = [strip_width // k for k in FACTORS]
        self.two = [(0, r, c) for r in range(self.rows[0]) for c in range(self.columns[0] + 2)]
        self.rest = [
            (s, r, c) for s in (1, 2) for r in range(self.rows[s]) for c in range(self.columns[s] + 2)
        ]
        self.n_two = round_up(len(self.two), 8)
        self.n_rest = round_up(len(self.rest), 8)
        self.two += [None] * (self.n_two - len(self.two))
        self.rest += [None] * (self.n_rest - len(self.rest))
        self.chunks_two = channels[0] // LANES
        self.chunks_rest = width // LANES
        self.coarse = [r * c * owners for r, c in zip(self.rows, self.columns)]
        self.rest_at = self.chunks_two * self.n_two
        self.slice_at = self.rest_at + self.chunks_rest * self.n_rest
        self.slice_width = channels[2] // owners
        self.sent = self.slice_at + round_up(self.coarse[2], 8)
        self.per_owner = round_up(self.n_two + self.n_rest, 16)
        self.positions = self.two + self.rest
        self.positions += [None] * (self.per_owner - len(self.positions))


def axis_weights(fine_count, factor):
    matrix = np.zeros((fine_count, fine_count // factor + 2), np.float32)
    for fine in range(fine_count):
        base, phase = divmod(fine, factor)
        offset = (phase + 0.5) / factor - 0.5
        if offset < 0:
            matrix[fine, base] += -offset
            matrix[fine, base + 1] += 1.0 + offset
        else:
            matrix[fine, base + 1] += 1.0 - offset
            matrix[fine, base + 2] += offset
    return matrix


def clamp_rows(matrix):
    folded = matrix[:, 1:-1].copy()
    folded[:, 0] += matrix[:, 0]
    folded[:, -1] += matrix[:, -1]
    return folded


def window_matrices(plan):
    owners, strip_width = plan.owners, plan.strip_width
    block_rows = plan.depth * 8
    fine_rows = owners * block_rows
    whole = np.zeros((fine_rows, strip_width, owners, plan.per_owner), np.float32)
    row_mats = [clamp_rows(axis_weights(fine_rows, k)) for k in FACTORS]
    col_mats = [axis_weights(strip_width, k) for k in FACTORS]
    for owner in range(owners):
        for index, entry in enumerate(plan.positions):
            if entry is not None:
                section, row, column = entry
                at = owner * plan.rows[section] + row
                whole[:, :, owner, index] = np.outer(
                    row_mats[section][:, at], col_mats[section][:, column]
                )
    up, down = [], []
    for owner in (0, 1, owners - 1):
        start = min(max(owner - 1, 0), owners - 3)
        rows = slice(owner * block_rows, (owner + 1) * block_rows)
        up.append(
            whole[rows, :, start : start + 3].reshape(block_rows * strip_width, 3 * plan.per_owner)
        )
        window = block_rows + 8
        low = min(max(owner * block_rows - 4, 0), fine_rows - window)
        piece = whole[low : low + window, :, owner]
        down.append(piece.reshape(window * strip_width, plan.per_owner).T)
    return np.stack(up).astype(BF16), np.stack(down).astype(BF16)


def selection(strip_map, plan, entries, sections):
    as_int = functools.partial(np.array, dtype=np.int32)
    strips = plan.owners
    offsets, at = {}, 0
    for s in sections:
        offsets[s] = at
        at += plan.coarse[s]
    start, base, span, limit = [], [], [], []
    for entry in entries:
        if entry is None:
            start.append(-1)
            base.append(0)
            span.append(0)
            limit.append(0)
            continue
        section, row, column = entry
        start.append(offsets[section] + row * plan.columns[section] * strips)
        base.append(column - 1)
        span.append(plan.columns[section])
        limit.append(strips * plan.columns[section] - 1)
    column = jnp.clip(strip_map[:, None] * as_int(span) + as_int(base), 0, as_int(limit))
    target = (column + as_int(start)).reshape(-1)
    places = np.arange(at, dtype=np.int32)
    pick = (target[:, None] == places[None]).astype(BF16)
    fold = (places[:, None] == target[None]).astype(BF16)
    return pick, fold


def contract(left, right, left_dim, right_dim):
    return lax.dot_general(
        left, right, (((left_dim,), (right_dim,)), ((), ())), preferred_element_type=F32
    )


def put_pieces(ref, at, values, count):
    owners = ref.shape[0]
    for piece in range(values.shape[1] // LANES):
        part = values[:, piece * LANES : (piece + 1) * LANES]
        ref[:, at + piece * count : at + (piece + 1) * count, :] = part.reshape(owners, count, LANES)


def take_pieces(ref, at, pieces, count):
    owners = ref.shape[0]
    return jnp.concatenate(
        [
            ref[:, at + p * count : at + (p + 1) * count, :].reshape(owners * count, LANES)
            for p in range(pieces)
        ],
        axis=1,
    )


def pack_kernel(plan, two_ref, three_ref, four_ref, l3_ref, l4_ref, pick_two_ref, pick_rest_ref, out_ref):
    picked = contract(pick_two_ref[...], two_ref[...], 1, 0).astype(BF16)
    put_pieces(out_ref, 0, picked, plan.n_two)
    projected = jnp.concatenate(
        [
            contract(three_ref[...], l3_ref[...], 1, 0).astype(BF16),
            contract(four_ref[...], l4_ref[...], 1, 0).astype(BF16),
        ]
    )
    picked = contract(pick_rest_ref[...], projected, 1, 0).astype(BF16)
    put_pieces(out_ref, plan.rest_at, picked, plan.n_rest)
    count = four_ref.shape[0]
    for owner in range(plan.owners):
        part = four_ref[:, owner * plan.slice_width : (owner + 1) * plan.slice_width]
        fill = jnp.zeros((count, LANES - plan.slice_width), BF16)
        out_ref[owner, plan.slice_at : plan.slice_at + count, :] = jnp.concatenate([part, fill], axis=1)


def put_parts(core, keep_ref, give_ref, at, part_ref):
    owners = 2 * keep_ref.shape[0]
    height = part_ref.shape[0] // owners
    for owner in range(owners):
        rows = part_ref[owner * height : (owner + 1) * height, :].astype(BF16)

        @pl.when(core == owner % 2)
        def _():
            keep_ref[owner // 2, at : at + height, :] = rows

        @pl.when(core != owner % 2)
        def _():
            give_ref[owner // 2, at : at + height, :] = rows


def strip_kernel(
    plan,
    core_ref,
    up_ref,
    down_ref,
    arrived_ref,
    fine_ref,
    cot_ref,
    l1_ref,
    l2_ref,
    join_ref,
    grad_fine_ref,
    back_ref,
    keep_a_ref,
    give_a_ref,
    keep_b_ref,
    give_b_ref,
    coarse_ref,
    hidden_ref,
    joined_grad_ref,
    two_grad_ref,
    join_part_ref,
    one_part_ref,
    two_part_ref,
):
    owners, n_two, n_rest, per_owner = plan.owners, plan.n_two, plan.n_rest, plan.per_owner
    core = core_ref[0]
    block = up_ref.shape[1]
    reach = up_ref.shape[2]
    window = down_ref.shape[2]
    total = cot_ref.shape[0]
    width = plan.width

    def variant(owner):
        return jnp.where(owner == 0, 0, jnp.where(owner == owners - 1, 2, 1))

    features = take_pieces(arrived_ref, 0, plan.chunks_two, n_two)
    projected = contract(features, l2_ref[...], 1, 0).astype(BF16).reshape(owners, n_two, width)
    rest = take_pieces(arrived_ref, plan.rest_at, plan.chunks_rest, n_rest).reshape(owners, n_rest, width)
    tail = per_owner - n_two - n_rest
    filled = [projected, rest] + ([jnp.zeros((owners, tail, width), BF16)] if tail else [])
    coarse_ref[...] = jnp.concatenate(filled, axis=1).reshape(owners * per_owner, width)

    @pl.loop(0, owners)
    def _(owner):
        start = pl.multiple_of(jnp.clip(owner - 1, 0, owners - 3) * per_owner, 16)
        rows = pl.ds(pl.multiple_of(owner * block, block), block)
        joined = contract(fine_ref[rows, :], l1_ref[...], 1, 0)
        joined += contract(up_ref[variant(owner)], coarse_ref[pl.ds(start, reach), :], 1, 0)
        gate = 0.5 + 0.5 * jnp.tanh(0.5 * joined)
        hidden = joined * gate
        hidden_ref[rows, :] = hidden.astype(BF16)
        slope = gate + hidden * (1.0 - gate)
        hidden_grad = contract(cot_ref[rows, :], join_ref[...], 1, 1)
        joined_grad = (hidden_grad * slope).astype(BF16)
        joined_grad_ref[rows, :] = joined_grad
        grad_fine_ref[rows, :] = contract(joined_grad, l1_ref[...], 1, 1).astype(BF16)

    @pl.loop(0, owners)
    def _(owner):
        low = pl.multiple_of(jnp.clip(owner * block - 32, 0, total - window), 32)
        strip_grad = contract(
            down_ref[variant(owner)], joined_grad_ref[pl.ds(low, window), :], 1, 0
        ).astype(BF16)
        two_grad_ref[owner] = strip_grad[:n_two]
        for piece in range(plan.chunks_rest):
            at = plan.rest_at + piece * n_rest
            back_ref[owner, at : at + n_rest, :] = strip_grad[
                n_two : n_two + n_rest, piece * LANES : (piece + 1) * LANES
            ]

    two_grad = two_grad_ref[...].reshape(owners * n_two, width)
    put_pieces(back_ref, 0, contract(two_grad, l2_ref[...], 1, 1).astype(BF16), n_two)
    join_part_ref[...] = contract(cot_ref[...], hidden_ref[...], 0, 0)
    one_part_ref[...] = contract(fine_ref[...], joined_grad_ref[...], 0, 0)
    two_part_ref[...] = contract(features, two_grad, 0, 0)
    put_parts(core, keep_a_ref, give_a_ref, 0, join_part_ref)
    two_height = two_part_ref.shape[0] // owners
    put_parts(core, keep_b_ref, give_b_ref, 0, two_part_ref)
    put_parts(core, keep_b_ref, give_b_ref, two_height, one_part_ref)
    used = two_height + one_part_ref.shape[0] // owners
    if used < keep_b_ref.shape[1]:
        fill = jnp.zeros((owners // 2, keep_b_ref.shape[1] - used, width), BF16)
        keep_b_ref[:, used:, :] = fill
        give_b_ref[:, used:, :] = fill


def fold_kernel(plan, core_ref, returned_ref, fold_ref, three_ref, g3_ref, g4_ref, keep_a_ref, give_a_ref, keep_b_ref, give_b_ref, part_ref):
    core = core_ref[0]
    rest = take_pieces(returned_ref, plan.rest_at, plan.chunks_rest, plan.n_rest)
    folded = contract(fold_ref[...], rest, 1, 0).astype(BF16)
    count = three_ref.shape[0]
    g3_ref[...] = folded[:count]
    g4_ref[...] = folded[count:]
    part_ref[...] = contract(three_ref[...], folded[:count], 0, 0)
    owners = plan.owners
    height = part_ref.shape[0] // owners
    half = height // 2
    for owner in range(owners):
        rows = part_ref[owner * height : (owner + 1) * height, :].astype(BF16)

        @pl.when(core == owner % 2)
        def _():
            keep_a_ref[owner // 2] = rows[:half]
            keep_b_ref[owner // 2] = rows[half:]

        @pl.when(core != owner % 2)
        def _():
            give_a_ref[owner // 2] = rows[:half]
            give_b_ref[owner // 2] = rows[half:]


def section_kernel(plan, returned_ref, fold_ref, g3_ref, g4_ref, l3_ref, l4_ref, two_ref, three_ref, four_ref):
    features = take_pieces(returned_ref, 0, plan.chunks_two, plan.n_two)
    two_ref[...] = contract(fold_ref[...], features, 1, 0).astype(BF16)
    three_ref[...] = contract(g3_ref[...], l3_ref[...], 1, 1).astype(BF16)
    four_ref[...] = contract(g4_ref[...], l4_ref[...], 1, 1).astype(BF16)


def swap(values, bit):
    owners = lax.axis_size("row")
    return lax.ppermute(values, "row", [(i, i ^ (1 << bit)) for i in range(owners)])


def plus(left, right):
    return (left.astype(F32) + right.astype(F32)).astype(BF16)


class Halving:
    def __init__(self, values, order):
        bits = len(order)
        self.values = values.reshape((2,) * bits + values.shape[1:])
        self.left = sorted(order, reverse=True)
        self.order = list(order)

    def step(self):
        bit = self.order.pop(0)
        axis = self.left.index(bit)
        self.left.pop(axis)
        mine = (lax.axis_index("row") >> bit) & 1
        keep = lax.dynamic_index_in_dim(self.values, mine, axis, keepdims=False)
        give = lax.dynamic_index_in_dim(self.values, 1 - mine, axis, keepdims=False)
        self.values = plus(keep, swap(give, bit))


def reduce_pair(first, second, bits):
    orders = list(range(1, bits)), list(range(1, bits))
    if bits > 2:
        orders[1][0], orders[1][1] = orders[1][1], orders[1][0]
    chains = [Halving(plus(keep, swap(give, 0)), order) for (keep, give), order in zip((first, second), orders)]
    for _ in range(1, bits):
        for chain in chains:
            chain.step()
    return [chain.values for chain in chains]


def gather_blocks(values, bits):
    stacked, pattern = values[None], np.zeros((1,), np.int32)
    for bit in bits:
        stacked = jnp.concatenate([stacked, swap(stacked, bit)])
        pattern = np.concatenate([pattern, pattern ^ (1 << bit)])
    return stacked, pattern


def shape_of(*dims, dtype=BF16):
    return jax.ShapeDtypeStruct(dims, dtype)


def body(
    fine_features,
    section_two,
    section_three,
    section_four,
    strip_map,
    lateral_one,
    lateral_two,
    lateral_three,
    lateral_four,
    join_weight,
    cotangent,
):
    owners = lax.axis_size("row")
    bits = owners.bit_length() - 1
    fine_height, strip_width, c1 = fine_features.shape
    width = join_weight.shape[0]
    sections = (section_two, section_three, section_four)
    channels = [s.shape[-1] for s in sections]
    plan = Plan(owners, section_four.shape[0], strip_width, channels, width)
    flats = [s.reshape(-1, s.shape[-1]) for s in sections]
    fine = fine_features.reshape(-1, c1)
    cot = cotangent.reshape(-1, width)
    total = fine.shape[0]
    me = lax.axis_index("row")
    core = (me & 1).astype(jnp.int32).reshape(1)
    pick_two, fold_two = selection(strip_map, plan, plan.two, (0,))
    pick_rest, fold_rest = selection(strip_map, plan, plan.rest, (1, 2))
    up, down = window_matrices(plan)
    exchange = functools.partial(lax.all_to_all, axis_name="row", split_axis=0, concat_axis=0, tiled=True)

    outgoing = pl.pallas_call(
        functools.partial(pack_kernel, plan),
        out_shape=shape_of(owners, plan.sent, LANES),
        in_specs=[VMEM] * 7,
        out_specs=VMEM,
        compiler_params=pltpu.CompilerParams(vmem_limit_bytes=32 * MEBI),
        name="pack",
    )(*flats, lateral_three, lateral_four, pick_two, pick_rest)
    arrived = exchange(outgoing)

    half = owners // 2
    heights = [width // owners, c1 // owners, channels[0] // owners]
    b_height = round_up(heights[1] + heights[2], 8)
    grad_fine, back, keep_a, give_a, keep_b, give_b = pl.pallas_call(
        functools.partial(strip_kernel, plan),
        out_shape=(
            shape_of(total, c1),
            shape_of(owners, plan.slice_at, LANES),
            shape_of(half, heights[0], width),
            shape_of(half, heights[0], width),
            shape_of(half, b_height, width),
            shape_of(half, b_height, width),
        ),
        in_specs=[SMEM] + [VMEM] * 8,
        out_specs=(VMEM,) * 6,
        scratch_shapes=[
            pltpu.VMEM((owners * plan.per_owner, width), BF16),
            pltpu.VMEM((total, width), BF16),
            pltpu.VMEM((total, width), BF16),
            pltpu.VMEM((owners, plan.n_two, width), BF16),
            pltpu.VMEM((width, width), F32),
            pltpu.VMEM((c1, width), F32),
            pltpu.VMEM((channels[0], width), F32),
        ],
        compiler_params=pltpu.CompilerParams(vmem_limit_bytes=48 * MEBI),
        cost_estimate=pl.CostEstimate(
            flops=5_000_000_000, bytes_accessed=9_000_000, transcendentals=total * width
        ),
        name="strip_work",
    )(core, up, down, arrived, fine, cot, lateral_one, lateral_two, join_weight)

    returned = exchange(back)
    early = reduce_pair((keep_a, give_a), (keep_b, give_b), bits)

    late_height = channels[1] // owners // 2
    g3, g4, keep_a, give_a, keep_b, give_b = pl.pallas_call(
        functools.partial(fold_kernel, plan),
        out_shape=(shape_of(plan.coarse[1], width), shape_of(plan.coarse[2], width))
        + (shape_of(half, late_height, width),) * 4,
        in_specs=[SMEM] + [VMEM] * 3,
        out_specs=(VMEM,) * 6,
        scratch_shapes=[pltpu.VMEM((channels[1], width), F32)],
        compiler_params=pltpu.CompilerParams(vmem_limit_bytes=32 * MEBI),
        name="fold_rest",
    )(core, returned, fold_rest, flats[1])
    gathered, pattern = gather_blocks(g4, list(range(bits))[::-1])
    late = reduce_pair((keep_a, give_a), (keep_b, give_b), bits)

    grads = pl.pallas_call(
        functools.partial(section_kernel, plan),
        out_shape=tuple(shape_of(*f.shape) for f in flats),
        in_specs=[VMEM] * 6,
        out_specs=(VMEM,) * 3,
        compiler_params=pltpu.CompilerParams(vmem_limit_bytes=32 * MEBI),
        cost_estimate=pl.CostEstimate(flops=500_000_000, bytes_accessed=6_000_000, transcendentals=0),
        name="section_grads",
    )(returned, fold_two, g3, g4, lateral_three, lateral_four)

    slices = arrived[:, plan.slice_at : plan.slice_at + plan.coarse[2], : plan.slice_width]
    slices = jnp.take(slices, me ^ pattern, axis=0).reshape(-1, plan.slice_width)
    grad_four_weight = contract(slices, gathered.reshape(-1, width), 0, 0)
    wide = [x.astype(F32) for x in early]
    return (
        grad_fine.reshape(fine_features.shape),
        *[g.reshape(s.shape) for g, s in zip(grads, sections)],
        wide[0].T,
        wide[1][heights[2] : heights[2] + heights[1]],
        wide[1][: heights[2]],
        jnp.concatenate(late, axis=0).astype(F32),
        grad_four_weight,
    )


def solution(mesh):
    fine_spec = P(None, ("group", "row"), None)
    coarse_spec = P("row", "group", None)
    weight_spec = P(("group", "row"), None)
    return jax.shard_map(
        body,
        mesh=mesh,
        in_specs=(fine_spec,) + (coarse_spec,) * 3 + (P("group"),) + (P(),) * 5 + (fine_spec,),
        out_specs=(fine_spec,) + (coarse_spec,) * 3 + (P("group", "row"),) + (weight_spec,) * 4,
        check_vma=False,
    )
```

```python
import functools

import jax
import jax.numpy as jnp
import numpy as np
from jax import lax
from jax.experimental import pallas as pl
from jax.experimental.pallas import tpu as pltpu
from jax.sharding import PartitionSpec as P

F32 = jnp.float32
BF16 = jnp.bfloat16
FACTORS = (2, 4, 8)
LANES = 128
VMEM = pl.BlockSpec(memory_space=pltpu.VMEM)
SMEM = pl.BlockSpec(memory_space=pltpu.SMEM)
ANY = pl.BlockSpec(memory_space=pl.ANY)
MEBI = 1024 * 1024
LIMIT = 60 * MEBI
ORDERS = ((0, 1), (1, 0))


def round_up(value, multiple):
    return -(-value // multiple) * multiple


class Plan:
    def __init__(self, owners, depth, strip_width, channels, width):
        self.owners, self.depth, self.strip_width = owners, depth, strip_width
        self.channels, self.width = channels, width
        self.rows = [depth * 8 // k for k in FACTORS]
        self.columns = [strip_width // k for k in FACTORS]
        self.coarse = [r * c * owners for r, c in zip(self.rows, self.columns)]
        self.entries, self.counts, self.starts = [], [], []
        at = 0
        for rows, columns in zip(self.rows, self.columns):
            entries = [(r, c) for r in range(rows) for c in range(columns + 2)]
            entries += [None] * (-len(entries) % 8)
            self.entries.append(entries)
            self.counts.append(len(entries))
            self.starts.append(at)
            at += len(entries)
        self.per_owner = round_up(at, 16)
        self.out_at, self.back_at = [], []
        self.sent = self.returned = 0
        for section in range(3):
            self.out_at.append(self.sent)
            self.back_at.append(self.returned)
            self.sent += self.counts[section] * (channels[section] // LANES)
            self.returned += self.counts[section] * (self.back_width(section) // LANES)

    def back_width(self, section):
        return self.channels[0] if section == 0 else self.width


def axis_weights(fine_count, factor):
    matrix = np.zeros((fine_count, fine_count // factor + 2), np.float32)
    for fine in range(fine_count):
        base, phase = divmod(fine, factor)
        offset = (phase + 0.5) / factor - 0.5
        if offset < 0:
            matrix[fine, base] += -offset
            matrix[fine, base + 1] += 1.0 + offset
        else:
            matrix[fine, base + 1] += 1.0 - offset
            matrix[fine, base + 2] += offset
    return matrix


def clamp_rows(matrix):
    folded = matrix[:, 1:-1].copy()
    folded[:, 0] += matrix[:, 0]
    folded[:, -1] += matrix[:, -1]
    return folded


def window_matrices(plan):
    owners, strip_width = plan.owners, plan.strip_width
    block_rows = plan.depth * 8
    fine_rows = owners * block_rows
    whole = np.zeros((fine_rows, strip_width, owners, plan.per_owner), np.float32)
    row_mats = [clamp_rows(axis_weights(fine_rows, k)) for k in FACTORS]
    col_mats = [axis_weights(strip_width, k) for k in FACTORS]
    for owner in range(owners):
        for section in range(3):
            for index, entry in enumerate(plan.entries[section]):
                if entry is not None:
                    at = owner * plan.rows[section] + entry[0]
                    whole[:, :, owner, plan.starts[section] + index] = np.outer(
                        row_mats[section][:, at], col_mats[section][:, entry[1]]
                    )
    up, down = [], []
    for owner in (0, 1, owners - 1):
        start = min(max(owner - 1, 0), owners - 3)
        rows = slice(owner * block_rows, (owner + 1) * block_rows)
        up.append(
            whole[rows, :, start : start + 3].reshape(block_rows * strip_width, 3 * plan.per_owner)
        )
        window = block_rows + 8
        low = min(max(owner * block_rows - 4, 0), fine_rows - window)
        piece = whole[low : low + window, :, owner]
        down.append(piece.reshape(window * strip_width, plan.per_owner).T)
    return np.stack(up).astype(BF16), np.stack(down).astype(BF16)


def entry_tables(plan, section):
    entries, columns = plan.entries[section], plan.columns[section]
    start = [-(1 << 20) if e is None else e[0] * columns * plan.owners for e in entries]
    offset = [0 if e is None else e[1] - 1 for e in entries]
    return np.array(start, np.int32), np.array(offset, np.int32)


def fold_matrix(strip_map, plan, section):
    start, offset = entry_tables(plan, section)
    columns = plan.columns[section]
    column = jnp.clip(strip_map[:, None] * columns + offset, 0, plan.owners * columns - 1)
    target = (column + start).reshape(-1)
    places = np.arange(plan.coarse[section], dtype=np.int32)
    return (places[:, None] == target[None]).astype(BF16)


def contract(left, right, left_dim, right_dim):
    return lax.dot_general(
        left, right, (((left_dim,), (right_dim,)), ((), ())), preferred_element_type=F32
    )


def put_pieces(ref, at, values, count):
    owners = ref.shape[0]
    for piece in range(values.shape[1] // LANES):
        part = values[:, piece * LANES : (piece + 1) * LANES]
        ref[:, at + piece * count : at + (piece + 1) * count, :] = part.reshape(owners, count, LANES)


def take_pieces(ref, at, pieces, count):
    owners = ref.shape[0]
    return jnp.concatenate(
        [
            ref[:, at + p * count : at + (p + 1) * count, :].reshape(owners * count, LANES)
            for p in range(pieces)
        ],
        axis=1,
    )


def copies_in(pairs, sem_ref):
    copies = [pltpu.make_async_copy(src, dst, sem_ref.at[i]) for i, (src, dst) in enumerate(pairs)]
    for copy in copies:
        copy.start()
    return copies


def entry_vectors(plan, section, shape):
    entry = lax.broadcasted_iota(jnp.int32, shape, 0)
    columns = plan.columns[section]
    span = columns + 2
    scale = -(-65536 // span)
    assert all((q * scale) >> 16 == q // span for q in range(shape[0]))
    row = (entry * scale) >> 16
    start = jnp.where(row < plan.rows[section], row * (columns * plan.owners), -(1 << 20))
    return start, entry - row * span - 1


def pack_kernel(plan, map_ref, *refs):
    sources, out_ref = refs[:3], refs[3]
    held, picks, sem_ref = refs[4:7], refs[7:10], refs[10]
    copies = copies_in(list(zip(sources, held)), sem_ref)
    for section in range(3):
        columns, count, places = plan.columns[section], plan.counts[section], plan.coarse[section]
        start, offset = entry_vectors(plan, section, (count, min(LANES, places)))
        lane = lax.broadcasted_iota(jnp.int32, start.shape, 1) - start
        for device in range(plan.owners):
            column = jnp.clip(map_ref[device] * columns + offset, 0, plan.owners * columns - 1)
            ahead = lane - column
            for at in range(0, places, LANES):
                picks[section][device, :, at : at + LANES] = jnp.where(ahead == -at, 1.0, 0.0).astype(BF16)
    for section in range(3):
        count = plan.counts[section]
        pick = picks[section][...].reshape(plan.owners * count, plan.coarse[section])
        copies[section].wait()
        chosen = contract(pick, held[section][...], 1, 0).astype(BF16)
        put_pieces(out_ref, plan.out_at[section], chosen, count)


def put_parts(part_refs, even_refs, odd_refs):
    owners = 2 * even_refs[0].shape[0]
    for owner in range(owners):
        refs = (even_refs, odd_refs)[owner % 2]
        index, at = 0, 0
        for part_ref in part_refs:
            height = part_ref.shape[0] // owners
            done = 0
            while done < height:
                if at == refs[index].shape[1]:
                    index, at = index + 1, 0
                count = min(height - done, refs[index].shape[1] - at)
                first = owner * height + done
                refs[index][owner // 2, at : at + count, :] = part_ref[first : first + count, :].astype(BF16)
                done += count
                at += count
        if at < refs[index].shape[1]:
            fill = jnp.zeros((refs[index].shape[1] - at, refs[index].shape[2]), BF16)
            refs[index][owner // 2, at:, :] = fill


def ahead_kernel(*refs):
    sources, outs = refs[:4], refs[4:6]
    held, stage, in_sem, out_sem = refs[6:10], refs[10:12], refs[12], refs[13]
    l1_ref, fine_ref, join_ref, cot_ref = held
    copies = copies_in(list(zip(sources, held)), in_sem)
    copies[0].wait()
    copies[1].wait()
    stage[0][...] = contract(fine_ref[...], l1_ref[...], 1, 0)
    first = pltpu.make_async_copy(stage[0], outs[0], out_sem.at[0])
    first.start()
    copies[2].wait()
    copies[3].wait()
    stage[1][...] = contract(cot_ref[...], join_ref[...], 1, 1)
    second = pltpu.make_async_copy(stage[1], outs[1], out_sem.at[1])
    second.start()
    first.wait()
    second.wait()


def strip_kernel(plan, turns, chains, core_ref, *refs):
    sent = 2 + 2 * chains
    sources, outs, held = refs[:11], refs[11 : 11 + sent], refs[11 + sent : 22 + sent]
    stage, refs = refs[22 + sent : 22 + 2 * sent], refs[22 + 2 * sent :]
    arrived_ref, l2_ref, l3_ref, l4_ref, up_ref, down_ref = held[:6]
    straight_ref, hidden_grad_ref, cot_ref, fine_ref, l1_ref = held[6:]
    grad_fine_ref, back_ref = stage[:2]
    coarse_ref, hidden_ref, joined_grad_ref = refs[:3]
    grad_refs, join_part_ref, one_part_ref = refs[3:6], refs[6], refs[7]
    part_refs, sem_ref, in_sem, turn_sem = refs[8:11], refs[11], refs[12], refs[13]
    lateral_refs = (l2_ref, l3_ref, l4_ref)
    owners, per_owner, width = plan.owners, plan.per_owner, plan.width
    core = core_ref[0]
    block = up_ref.shape[1]
    reach = up_ref.shape[2]
    window = down_ref.shape[2]
    total = cot_ref.shape[0]
    group = owners // turns
    copies = copies_in(list(zip(sources[:6], held[:6])), in_sem)
    turn_copies = []
    for turn in range(turns):
        many = pl.ds(turn * group * block, group * block)
        for which in (0, 1):
            copy = pltpu.make_async_copy(
                sources[6 + which].at[many], held[6 + which].at[many], turn_sem.at[which, turn]
            )
            copy.start()
            turn_copies.append(copy)
    late_copies = []
    for index in (8, 9, 10):
        copy = pltpu.make_async_copy(sources[index], held[index], in_sem.at[index - 2])
        copy.start()
        late_copies.append(copy)

    def leave(index):
        copy = pltpu.make_async_copy(stage[index], outs[index], sem_ref.at[index])
        copy.start()
        return copy

    def features(section):
        return take_pieces(
            arrived_ref, plan.out_at[section], plan.channels[section] // LANES, plan.counts[section]
        )

    copies[0].wait()
    projected = []
    for section in range(3):
        copies[1 + section].wait()
        product = contract(features(section), lateral_refs[section][...], 1, 0).astype(BF16)
        projected.append(product.reshape(owners, plan.counts[section], width))
    tail = per_owner - sum(plan.counts)
    if tail:
        projected.append(jnp.zeros((owners, tail, width), BF16))
    coarse_ref[...] = jnp.concatenate(projected, axis=1).reshape(owners * per_owner, width)
    copies[4].wait()
    copies[5].wait()

    for turn in range(turns):
        turn_copies[2 * turn].wait()
        turn_copies[2 * turn + 1].wait()
        for owner in range(turn * group, (turn + 1) * group):
            kind = 0 if owner == 0 else 2 if owner == owners - 1 else 1
            start = min(max(owner - 1, 0), owners - 3) * per_owner
            rows = slice(owner * block, (owner + 1) * block)
            joined = straight_ref[rows, :] + contract(
                up_ref[kind], coarse_ref[start : start + reach, :], 1, 0
            )
            gate = 0.5 + 0.5 * jnp.tanh(0.5 * joined)
            hidden = joined * gate
            hidden_ref[rows, :] = hidden.astype(BF16)
            slope = gate + hidden * (1.0 - gate)
            joined_grad_ref[rows, :] = (hidden_grad_ref[rows, :] * slope).astype(BF16)

    for owner in range(owners):
        kind = 0 if owner == 0 else 2 if owner == owners - 1 else 1
        low = min(max(owner * block - 32, 0), total - window)
        strip_grad = contract(down_ref[kind], joined_grad_ref[low : low + window, :], 1, 0).astype(BF16)
        for section in range(3):
            at = plan.starts[section]
            grad_refs[section][owner] = strip_grad[at : at + plan.counts[section]]

    strip_grads = [
        ref[...].reshape(owners * count, width) for ref, count in zip(grad_refs, plan.counts)
    ]
    put_pieces(back_ref, 0, contract(strip_grads[0], l2_ref[...], 1, 1).astype(BF16), plan.counts[0])
    for section in (1, 2):
        put_pieces(back_ref, plan.back_at[section], strip_grads[section], plan.counts[section])
    leaving = [leave(1)]
    for section in range(3):
        part_refs[section][...] = contract(features(section), strip_grads[section], 0, 0)
    for copy in late_copies:
        copy.wait()
    join_part_ref[...] = contract(cot_ref[...], hidden_ref[...], 0, 0)
    one_part_ref[...] = contract(fine_ref[...], joined_grad_ref[...], 0, 0)

    kept, given = stage[2 : 2 + chains], stage[2 + chains :]
    ordered_parts = (join_part_ref, *part_refs, one_part_ref)

    @pl.when(core == 0)
    def _():
        put_parts(ordered_parts, kept, given)

    @pl.when(core != 0)
    def _():
        put_parts(ordered_parts, given, kept)

    leaving += [leave(index) for index in range(2, len(stage))]
    grad_fine_ref[...] = contract(joined_grad_ref[...], l1_ref[...], 1, 1).astype(BF16)
    leaving.append(leave(0))
    for copy in leaving:
        copy.wait()


def section_kernel(plan, *refs):
    sources, outs, held, sem_ref = refs[:6], refs[6:9], refs[9:15], refs[15]
    copies = copies_in(list(zip(sources, held)), sem_ref)
    returned_ref, folds, laterals = held[0], held[1:4], held[4:6]
    copies[0].wait()
    for section in range(3):
        arrived = take_pieces(
            returned_ref, plan.back_at[section], plan.back_width(section) // LANES, plan.counts[section]
        )
        copies[1 + section].wait()
        folded = contract(folds[section][...], arrived, 1, 0).astype(BF16)
        if section > 0:
            copies[3 + section].wait()
            folded = contract(folded, laterals[section - 1][...], 1, 1).astype(BF16)
        outs[section][...] = folded


def swap(values, bit):
    owners = lax.axis_size("row")
    return lax.ppermute(values, "row", [(i, i ^ (1 << bit)) for i in range(owners)])


def plus(left, right):
    return (left.astype(F32) + right.astype(F32)).astype(BF16)


class Halving:
    def __init__(self, values, order):
        bits = len(order)
        self.values = values.reshape((2,) * bits + values.shape[1:])
        self.left = sorted(order, reverse=True)
        self.order = list(order)

    def step(self):
        bit = self.order.pop(0)
        axis = self.left.index(bit)
        self.left.pop(axis)
        mine = (lax.axis_index("row") >> bit) & 1
        keep = lax.dynamic_index_in_dim(self.values, mine, axis, keepdims=False)
        give = lax.dynamic_index_in_dim(self.values, 1 - mine, axis, keepdims=False)
        self.values = plus(keep, swap(give, bit))


def reduce_chains(kept, given, bits):
    chains = []
    for keep, give, order in zip(kept, given, ORDERS):
        rest = list(range(1, bits))
        rest[: len(order)] = [rest[i] for i in order]
        chains.append(Halving(plus(keep, swap(give, 0)), rest))
    for _ in range(1, bits):
        for chain in chains:
            chain.step()
    return [chain.values for chain in chains]


def shape_of(*dims, dtype=BF16):
    return jax.ShapeDtypeStruct(dims, dtype)


def body(
    fine_features,
    section_two,
    section_three,
    section_four,
    strip_map,
    lateral_one,
    lateral_two,
    lateral_three,
    lateral_four,
    join_weight,
    cotangent,
):
    owners = lax.axis_size("row")
    bits = owners.bit_length() - 1
    fine_height, strip_width, c1 = fine_features.shape
    width = join_weight.shape[0]
    sections = (section_two, section_three, section_four)
    channels = [s.shape[-1] for s in sections]
    plan = Plan(owners, section_four.shape[0], strip_width, channels, width)
    flats = [s.reshape(-1, s.shape[-1]) for s in sections]
    fine = fine_features.reshape(-1, c1)
    cot = cotangent.reshape(-1, width)
    total = fine.shape[0]
    me = lax.axis_index("row")
    core = (me & 1).astype(jnp.int32).reshape(1)
    up, down = window_matrices(plan)
    exchange = functools.partial(lax.all_to_all, axis_name="row", split_axis=0, concat_axis=0, tiled=True)

    outgoing = pl.pallas_call(
        functools.partial(pack_kernel, plan),
        out_shape=shape_of(owners, plan.sent, LANES),
        in_specs=[SMEM] + [ANY] * 3,
        out_specs=VMEM,
        scratch_shapes=[pltpu.VMEM(f.shape, BF16) for f in flats]
        + [pltpu.VMEM((owners, count, places), BF16) for count, places in zip(plan.counts, plan.coarse)]
        + [pltpu.SemaphoreType.DMA((3,))],
        compiler_params=pltpu.CompilerParams(vmem_limit_bytes=LIMIT),
        name="pack",
    )(strip_map, *flats)
    arrived = exchange(outgoing)

    half = owners // 2
    heights = [x // owners for x in (width, *channels, c1)]
    chains = len(ORDERS)
    tall = round_up(sum(heights), 8)
    cuts = [round_up(tall * c // chains, 8) for c in range(chains)] + [tall]
    chain_heights = [high - low for low, high in zip(cuts, cuts[1:])]
    early = (lateral_one, fine, join_weight, cot)
    straight, hidden_grad = pl.pallas_call(
        ahead_kernel,
        out_shape=(shape_of(total, width, dtype=F32),) * 2,
        in_specs=[ANY] * 4,
        out_specs=(ANY,) * 2,
        scratch_shapes=[pltpu.VMEM(x.shape, BF16) for x in early]
        + [pltpu.VMEM((total, width), F32)] * 2
        + [pltpu.SemaphoreType.DMA((4,)), pltpu.SemaphoreType.DMA((2,))],
        compiler_params=pltpu.CompilerParams(vmem_limit_bytes=LIMIT),
        cost_estimate=pl.CostEstimate(
            flops=4 * total * width * (width + c1), bytes_accessed=14_000_000, transcendentals=0
        ),
        name="ahead",
    )(*early)
    operands = (
        arrived,
        lateral_two,
        lateral_three,
        lateral_four,
        up,
        down,
        straight,
        hidden_grad,
        cot,
        fine,
        lateral_one,
    )
    stage = (shape_of(total, c1), shape_of(owners, plan.returned, LANES))
    stage += tuple(shape_of(half, height, width) for height in chain_heights) * 2
    grad_fine, back, *halves = pl.pallas_call(
        functools.partial(strip_kernel, plan, 4, chains),
        out_shape=stage,
        in_specs=[SMEM] + [ANY] * 11,
        out_specs=(ANY,) * len(stage),
        scratch_shapes=[pltpu.VMEM(x.shape, x.dtype) for x in operands + stage]
        + [
            pltpu.VMEM((owners * plan.per_owner, width), BF16),
            pltpu.VMEM((total, width), BF16),
            pltpu.VMEM((total, width), BF16),
        ]
        + [pltpu.VMEM((owners, count, width), BF16) for count in plan.counts]
        + [pltpu.VMEM((x, width), F32) for x in (width, c1, *channels)]
        + [
            pltpu.SemaphoreType.DMA((len(stage),)),
            pltpu.SemaphoreType.DMA((9,)),
            pltpu.SemaphoreType.DMA((2, 4)),
        ],
        compiler_params=pltpu.CompilerParams(vmem_limit_bytes=LIMIT),
        cost_estimate=pl.CostEstimate(
            flops=4_000_000_000, bytes_accessed=9_000_000, transcendentals=total * width
        ),
        name="strip_work",
    )(core, *operands)

    returned = exchange(back)
    summed = reduce_chains(halves[:chains], halves[chains:], bits)
    summed = jnp.concatenate(summed, axis=0).astype(F32)
    ends = np.cumsum([0] + heights).tolist()
    weight_grads = [summed[low:high] for low, high in zip(ends, ends[1:])]

    operands = (
        returned,
        *[fold_matrix(strip_map, plan, section) for section in range(3)],
        lateral_three,
        lateral_four,
    )
    grads = pl.pallas_call(
        functools.partial(section_kernel, plan),
        out_shape=tuple(shape_of(*f.shape) for f in flats),
        in_specs=[ANY] * 6,
        out_specs=(VMEM,) * 3,
        scratch_shapes=[pltpu.VMEM(x.shape, BF16) for x in operands] + [pltpu.SemaphoreType.DMA((6,))],
        compiler_params=pltpu.CompilerParams(vmem_limit_bytes=LIMIT),
        cost_estimate=pl.CostEstimate(flops=500_000_000, bytes_accessed=6_000_000, transcendentals=0),
        name="section_grads",
    )(*operands)

    return (
        grad_fine.reshape(fine_features.shape),
        *[g.reshape(s.shape) for g, s in zip(grads, sections)],
        weight_grads[0].T,
        weight_grads[4],
        *weight_grads[1:4],
    )


def solution(mesh):
    fine_spec = P(None, ("group", "row"), None)
    coarse_spec = P("row", "group", None)
    weight_spec = P(("group", "row"), None)
    return jax.shard_map(
        body,
        mesh=mesh,
        in_specs=(fine_spec,) + (coarse_spec,) * 3 + (P("group"),) + (P(),) * 5 + (fine_spec,),
        out_specs=(fine_spec,) + (coarse_spec,) * 3 + (P("group", "row"),) + (weight_spec,) * 4,
        check_vma=False,
    )
```

```python
import functools

import jax
import jax.numpy as jnp
import numpy as np
from jax import lax
from jax.experimental import pallas as pl
from jax.experimental.pallas import tpu as pltpu
from jax.sharding import PartitionSpec as P

F32 = jnp.float32
BF16 = jnp.bfloat16
FACTORS = (2, 4, 8)
LANES = 128
VMEM = pl.BlockSpec(memory_space=pltpu.VMEM)
SMEM = pl.BlockSpec(memory_space=pltpu.SMEM)
ANY = pl.BlockSpec(memory_space=pl.ANY)
MEBI = 1024 * 1024
LIMIT = 62 * MEBI
SMALL = 62 * MEBI
TURNS = 4
CHAINS = 1


def round_up(value, multiple):
    return -(-value // multiple) * multiple


class Plan:
    def __init__(self, owners, depth, strip_width, channels, width):
        self.owners, self.depth, self.strip_width = owners, depth, strip_width
        self.channels, self.width = channels, width
        self.rows = [depth * 8 // k for k in FACTORS]
        self.columns = [strip_width // k for k in FACTORS]
        self.coarse = [r * c * owners for r, c in zip(self.rows, self.columns)]
        self.entries, self.counts, self.starts = [], [], []
        at = 0
        for rows, columns in zip(self.rows, self.columns):
            entries = [(r, c) for r in range(rows) for c in range(columns + 2)]
            entries += [None] * (-len(entries) % 8)
            self.entries.append(entries)
            self.counts.append(len(entries))
            self.starts.append(at)
            at += len(entries)
        self.per_owner = round_up(at, 16)
        self.out_at, self.back_at = [], []
        self.sent = self.returned = 0
        for section in range(3):
            self.out_at.append(self.sent)
            self.sent += self.counts[section] * (self.out_width(section) // LANES)
        for section in range(3):
            self.back_at.append(self.returned)
            self.returned += self.counts[section] * (self.back_width(section) // LANES)
        self.slice_at = self.sent
        self.slice_width = channels[2] // owners
        self.sent += self.coarse[2]

    def out_width(self, section):
        return self.channels[section] if section < 2 else self.width

    def back_width(self, section):
        return self.channels[0] if section == 0 else self.width


def axis_weights(fine_count, factor):
    matrix = np.zeros((fine_count, fine_count // factor + 2), np.float32)
    for fine in range(fine_count):
        base, phase = divmod(fine, factor)
        offset = (phase + 0.5) / factor - 0.5
        if offset < 0:
            matrix[fine, base] += -offset
            matrix[fine, base + 1] += 1.0 + offset
        else:
            matrix[fine, base + 1] += 1.0 - offset
            matrix[fine, base + 2] += offset
    return matrix


def clamp_rows(matrix):
    folded = matrix[:, 1:-1].copy()
    folded[:, 0] += matrix[:, 0]
    folded[:, -1] += matrix[:, -1]
    return folded


def window_matrices(plan):
    owners, strip_width = plan.owners, plan.strip_width
    block_rows = plan.depth * 8
    fine_rows = owners * block_rows
    whole = np.zeros((fine_rows, strip_width, owners, plan.per_owner), np.float32)
    row_mats = [clamp_rows(axis_weights(fine_rows, k)) for k in FACTORS]
    col_mats = [axis_weights(strip_width, k) for k in FACTORS]
    for owner in range(owners):
        for section in range(3):
            for index, entry in enumerate(plan.entries[section]):
                if entry is not None:
                    at = owner * plan.rows[section] + entry[0]
                    whole[:, :, owner, plan.starts[section] + index] = np.outer(
                        row_mats[section][:, at], col_mats[section][:, entry[1]]
                    )
    up, down = [], []
    for owner in (0, 1, owners - 1):
        start = min(max(owner - 1, 0), owners - 3)
        rows = slice(owner * block_rows, (owner + 1) * block_rows)
        up.append(
            whole[rows, :, start : start + 3].reshape(block_rows * strip_width, 3 * plan.per_owner)
        )
        window = block_rows + 8
        low = min(max(owner * block_rows - 4, 0), fine_rows - window)
        piece = whole[low : low + window, :, owner]
        down.append(piece.reshape(window * strip_width, plan.per_owner).T)
    return np.stack(up).astype(BF16), np.stack(down).astype(BF16)


def entry_tables(plan, section):
    entries, columns = plan.entries[section], plan.columns[section]
    start = [-(1 << 20) if e is None else e[0] * columns * plan.owners for e in entries]
    offset = [0 if e is None else e[1] - 1 for e in entries]
    return np.array(start, np.int32), np.array(offset, np.int32)


def fold_matrix(strip_map, plan, section):
    start, offset = entry_tables(plan, section)
    columns = plan.columns[section]
    column = jnp.clip(strip_map[:, None] * columns + offset, 0, plan.owners * columns - 1)
    target = (column + start).reshape(-1)
    places = np.arange(plan.coarse[section], dtype=np.int32)
    return (places[:, None] == target[None]).astype(BF16)


def contract(left, right, left_dim, right_dim):
    return lax.dot_general(
        left, right, (((left_dim,), (right_dim,)), ((), ())), preferred_element_type=F32
    )


def put_pieces(ref, at, values, count):
    owners = ref.shape[0]
    for piece in range(values.shape[1] // LANES):
        part = values[:, piece * LANES : (piece + 1) * LANES]
        ref[:, at + piece * count : at + (piece + 1) * count, :] = part.reshape(owners, count, LANES)


def take_pieces(ref, at, pieces, count):
    owners = ref.shape[0]
    return jnp.concatenate(
        [
            ref[:, at + p * count : at + (p + 1) * count, :].reshape(owners * count, LANES)
            for p in range(pieces)
        ],
        axis=1,
    )


def copies_in(pairs, sem_ref):
    copies = [pltpu.make_async_copy(src, dst, sem_ref.at[i]) for i, (src, dst) in enumerate(pairs)]
    for copy in copies:
        copy.start()
    return copies


def entry_vectors(plan, section, shape):
    entry = lax.broadcasted_iota(jnp.int32, shape, 0)
    columns = plan.columns[section]
    span = columns + 2
    scale = -(-65536 // span)
    assert all((q * scale) >> 16 == q // span for q in range(shape[0]))
    row = (entry * scale) >> 16
    start = jnp.where(row < plan.rows[section], row * (columns * plan.owners), -(1 << 20))
    return start, entry - row * span - 1


def pack_kernel(plan, map_ref, *refs):
    sources, out_ref = refs[:4], refs[4]
    held, picks, sem_ref = refs[5:9], refs[9:12], refs[12]
    copies = copies_in(list(zip(sources, held)), sem_ref)
    four_ref, l4_ref = held[2:]
    for section in range(3):
        columns, count, places = plan.columns[section], plan.counts[section], plan.coarse[section]
        start, offset = entry_vectors(plan, section, (count, min(LANES, places)))
        lane = lax.broadcasted_iota(jnp.int32, start.shape, 1) - start
        for device in range(plan.owners):
            column = jnp.clip(map_ref[device] * columns + offset, 0, plan.owners * columns - 1)
            ahead = lane - column
            for at in range(0, places, LANES):
                picks[section][device, :, at : at + LANES] = jnp.where(ahead == -at, 1.0, 0.0).astype(BF16)
    for section in range(3):
        count = plan.counts[section]
        pick = picks[section][...].reshape(plan.owners * count, plan.coarse[section])
        copies[section].wait()
        values = held[section][...]
        if section == 2:
            copies[3].wait()
            values = contract(values, l4_ref[...], 1, 0).astype(BF16)
        put_pieces(out_ref, plan.out_at[section], contract(pick, values, 1, 0).astype(BF16), count)
    count = plan.coarse[2]
    fill = jnp.zeros((count, LANES - plan.slice_width), BF16)
    for owner in range(plan.owners):
        part = four_ref[:, owner * plan.slice_width : (owner + 1) * plan.slice_width]
        out_ref[owner, plan.slice_at :, :] = jnp.concatenate([part, fill], axis=1)


def put_parts(part_refs, even_refs, odd_refs):
    owners = 2 * even_refs[0].shape[0]
    for owner in range(owners):
        refs = (even_refs, odd_refs)[owner % 2]
        index, at = 0, 0
        for part_ref in part_refs:
            height = part_ref.shape[0] // owners
            done = 0
            while done < height:
                if at == refs[index].shape[1]:
                    index, at = index + 1, 0
                count = min(height - done, refs[index].shape[1] - at)
                first = owner * height + done
                refs[index][owner // 2, at : at + count, :] = part_ref[first : first + count, :].astype(BF16)
                done += count
                at += count
        if at < refs[index].shape[1]:
            fill = jnp.zeros((refs[index].shape[1] - at, refs[index].shape[2]), BF16)
            refs[index][owner // 2, at:, :] = fill


def ahead_kernel(*refs):
    sources, outs = refs[:4], refs[4:6]
    held, stage, in_sem, out_sem = refs[6:10], refs[10:12], refs[12], refs[13]
    l1_ref, fine_ref, join_ref, cot_ref = held
    copies = copies_in(list(zip(sources, held)), in_sem)
    copies[0].wait()
    copies[1].wait()
    stage[0][...] = contract(fine_ref[...], l1_ref[...], 1, 0)
    first = pltpu.make_async_copy(stage[0], outs[0], out_sem.at[0])
    first.start()
    copies[2].wait()
    copies[3].wait()
    stage[1][...] = contract(cot_ref[...], join_ref[...], 1, 1)
    second = pltpu.make_async_copy(stage[1], outs[1], out_sem.at[1])
    second.start()
    first.wait()
    second.wait()


def take_features(plan, arrived_ref, section):
    return take_pieces(
        arrived_ref, plan.out_at[section], plan.out_width(section) // LANES, plan.counts[section]
    )


def strip_kernel(plan, turns, chains, core_ref, *refs):
    sent = 2 + 2 * chains
    sources, outs, held = refs[:10], refs[10 : 10 + sent], refs[10 + sent : 20 + sent]
    stage, refs = refs[20 + sent : 20 + 2 * sent], refs[20 + 2 * sent :]
    arrived_ref, l2_ref, l3_ref, up_ref, down_ref = held[:5]
    straight_ref, hidden_grad_ref, cot_ref, fine_ref, l1_ref = held[5:]
    grad_fine_ref, back_ref = stage[:2]
    coarse_ref, hidden_ref, joined_grad_ref = refs[:3]
    grad_refs = refs[3:6]
    join_part_ref, two_part_ref, three_part_ref, one_part_ref, out_sem, in_sem, turn_sem = refs[6:]
    owners, per_owner, width = plan.owners, plan.per_owner, plan.width
    core = core_ref[0]
    block = up_ref.shape[1]
    reach = up_ref.shape[2]
    window = down_ref.shape[2]
    total = cot_ref.shape[0]
    group = owners // turns
    copies = copies_in(list(zip(sources[:5], held[:5])), in_sem)
    turn_copies = []
    for turn in range(turns):
        many = pl.ds(turn * group * block, group * block)
        for which in (0, 1):
            copy = pltpu.make_async_copy(
                sources[5 + which].at[many], held[5 + which].at[many], turn_sem.at[which, turn]
            )
            copy.start()
            turn_copies.append(copy)
    late_copies = []
    for index in (7, 8, 9):
        copy = pltpu.make_async_copy(sources[index], held[index], in_sem.at[index - 2])
        copy.start()
        late_copies.append(copy)

    def leave(index):
        copy = pltpu.make_async_copy(stage[index], outs[index], out_sem.at[index])
        copy.start()
        return copy

    copies[0].wait()
    features = [
        take_pieces(arrived_ref, plan.out_at[section], plan.out_width(section) // LANES, plan.counts[section])
        for section in range(3)
    ]
    projected = []
    for section in range(3):
        product = features[section]
        if section < 2:
            copies[1 + section].wait()
            product = contract(product, (l2_ref, l3_ref)[section][...], 1, 0).astype(BF16)
        projected.append(product.reshape(owners, plan.counts[section], width))
    tail = per_owner - sum(plan.counts)
    if tail:
        projected.append(jnp.zeros((owners, tail, width), BF16))
    coarse_ref[...] = jnp.concatenate(projected, axis=1).reshape(owners * per_owner, width)
    copies[3].wait()
    copies[4].wait()

    for turn in range(turns):
        turn_copies[2 * turn].wait()
        turn_copies[2 * turn + 1].wait()
        for owner in range(turn * group, (turn + 1) * group):
            kind = 0 if owner == 0 else 2 if owner == owners - 1 else 1
            start = min(max(owner - 1, 0), owners - 3) * per_owner
            rows = slice(owner * block, (owner + 1) * block)
            joined = straight_ref[rows, :] + contract(
                up_ref[kind], coarse_ref[start : start + reach, :], 1, 0
            )
            gate = 0.5 + 0.5 * jnp.tanh(0.5 * joined)
            hidden = joined * gate
            hidden_ref[rows, :] = hidden.astype(BF16)
            slope = gate + hidden * (1.0 - gate)
            joined_grad_ref[rows, :] = (hidden_grad_ref[rows, :] * slope).astype(BF16)

    for owner in range(owners):
        kind = 0 if owner == 0 else 2 if owner == owners - 1 else 1
        low = min(max(owner * block - 32, 0), total - window)
        strip_grad = contract(down_ref[kind], joined_grad_ref[low : low + window, :], 1, 0)
        for section, ref in enumerate(grad_refs):
            at = plan.starts[section]
            ref[owner] = strip_grad[at : at + plan.counts[section]].astype(BF16)
    strip_grads = [ref[...].reshape(owners * count, width) for ref, count in zip(grad_refs, plan.counts)]
    for section in (1, 2):
        put_pieces(back_ref, plan.back_at[section], strip_grads[section], plan.counts[section])
    put_pieces(back_ref, 0, contract(strip_grads[0], l2_ref[...], 1, 1).astype(BF16), plan.counts[0])
    leaving = [leave(1)]
    two_part_ref[...] = contract(features[0], strip_grads[0], 0, 0)
    three_part_ref[...] = contract(features[1], strip_grads[1], 0, 0)
    for copy in late_copies:
        copy.wait()
    join_part_ref[...] = contract(cot_ref[...], hidden_ref[...], 0, 0)
    one_part_ref[...] = contract(fine_ref[...], joined_grad_ref[...], 0, 0)
    kept, given = stage[2 : 2 + chains], stage[2 + chains :]
    parts = (join_part_ref, two_part_ref, three_part_ref, one_part_ref)

    @pl.when(core == 0)
    def _():
        put_parts(parts, kept, given)

    @pl.when(core != 0)
    def _():
        put_parts(parts, given, kept)

    leaving += [leave(index) for index in range(2, sent)]
    grad_fine_ref[...] = contract(joined_grad_ref[...], l1_ref[...], 1, 1).astype(BF16)
    leaving.append(leave(0))
    for copy in leaving:
        copy.wait()


def finish_kernel(plan, chains, *refs):
    count = (len(refs) - 6) // 2
    sources, outs, held, sem_ref = refs[:count], refs[count : count + 5], refs[count + 5 : -1], refs[-1]
    copies = copies_in(list(zip(sources, held)), sem_ref)
    first = 2 * chains
    for copy in copies[:first]:
        copy.wait()
    total = jnp.concatenate(
        [held[2 * c][...].astype(F32) + held[2 * c + 1][...].astype(F32) for c in range(chains)]
    )
    join_ref, two_ref, three_ref, one_ref, four_ref = outs
    at = 0
    for ref in (join_ref, two_ref, three_ref, one_ref):
        ref[...] = total[at : at + ref.shape[0]]
        at += ref.shape[0]
    for copy in copies[first:]:
        copy.wait()
    slices_ref, pieces = held[first], held[first + 1 :]
    blocks = jnp.concatenate([piece[...] for piece in pieces])
    four_ref[...] = contract(slices_ref[...], blocks, 0, 0)[: four_ref.shape[0]]


def fold_kernel(plan, returned_ref, fold_ref, out_ref):
    arrived = take_pieces(returned_ref, plan.back_at[2], plan.back_width(2) // LANES, plan.counts[2])
    out_ref[...] = contract(fold_ref[...], arrived, 1, 0).astype(BF16)


def section_kernel(plan, *refs):
    sources, outs, held, sem_ref = refs[:6], refs[6:9], refs[9:15], refs[15]
    copies = copies_in(list(zip(sources, held)), sem_ref)
    returned_ref, folds, l3_ref, l4_ref, four_ref = held[0], held[1:3], held[3], held[4], held[5]
    copies[0].wait()
    for section in range(2):
        arrived = take_pieces(
            returned_ref, plan.back_at[section], plan.back_width(section) // LANES, plan.counts[section]
        )
        copies[1 + section].wait()
        folded = contract(folds[section][...], arrived, 1, 0).astype(BF16)
        if section == 1:
            copies[3].wait()
            folded = contract(folded, l3_ref[...], 1, 1).astype(BF16)
        outs[section][...] = folded
    copies[4].wait()
    copies[5].wait()
    outs[2][...] = contract(four_ref[...], l4_ref[...], 1, 1).astype(BF16)


def swap(values, bit):
    owners = lax.axis_size("row")
    return lax.ppermute(values, "row", [(i, i ^ (1 << bit)) for i in range(owners)])


def plus(left, right):
    return (left.astype(F32) + right.astype(F32)).astype(BF16)


class Halving:
    def __init__(self, values, order):
        bits = len(order)
        self.values = values.reshape((2,) * bits + values.shape[1:])
        self.left = sorted(order, reverse=True)
        self.order = list(order)

    def split(self):
        bit = self.order.pop(0)
        axis = self.left.index(bit)
        self.left.pop(axis)
        mine = (lax.axis_index("row") >> bit) & 1
        keep = lax.dynamic_index_in_dim(self.values, mine, axis, keepdims=False)
        give = lax.dynamic_index_in_dim(self.values, 1 - mine, axis, keepdims=False)
        return keep, give, bit

    def step(self, later=None):
        keep, give, bit = self.split()
        if later is not None:
            give, later = lax.optimization_barrier((give, later))
        if self.order:
            self.values = plus(keep, swap(give, bit))
        else:
            self.terms = keep, swap(give, bit)
        return later


def level_swaps(level):
    distances = [0]
    for bit in level:
        distances += [d ^ (1 << bit) for d in distances]
    return distances


def gather_level(stacked, level):
    owners = lax.axis_size("row")
    distances = level_swaps(level)[1:]
    return [stacked] + [lax.ppermute(stacked, "row", [(i, i ^ d) for i in range(owners)]) for d in distances]


def gather_pattern(levels):
    pattern = np.zeros((1,), np.int32)
    for level in levels:
        pattern = np.concatenate([pattern ^ d for d in level_swaps(level)])
    return pattern


def shape_of(*dims, dtype=BF16):
    return jax.ShapeDtypeStruct(dims, dtype)


def body(
    fine_features,
    section_two,
    section_three,
    section_four,
    strip_map,
    lateral_one,
    lateral_two,
    lateral_three,
    lateral_four,
    join_weight,
    cotangent,
):
    owners = lax.axis_size("row")
    bits = owners.bit_length() - 1
    fine_height, strip_width, c1 = fine_features.shape
    width = join_weight.shape[0]
    sections = (section_two, section_three, section_four)
    channels = [s.shape[-1] for s in sections]
    plan = Plan(owners, section_four.shape[0], strip_width, channels, width)
    flats = [s.reshape(-1, s.shape[-1]) for s in sections]
    fine = fine_features.reshape(-1, c1)
    cot = cotangent.reshape(-1, width)
    total = fine.shape[0]
    me = lax.axis_index("row")
    core = (me & 1).astype(jnp.int32).reshape(1)
    up, down = window_matrices(plan)
    exchange = functools.partial(lax.all_to_all, axis_name="row", split_axis=0, concat_axis=0, tiled=True)

    outgoing = pl.pallas_call(
        functools.partial(pack_kernel, plan),
        out_shape=shape_of(owners, plan.sent, LANES),
        in_specs=[SMEM] + [ANY] * 4,
        out_specs=VMEM,
        scratch_shapes=[pltpu.VMEM(x.shape, BF16) for x in (*flats, lateral_four)]
        + [pltpu.VMEM((owners, count, places), BF16) for count, places in zip(plan.counts, plan.coarse)]
        + [pltpu.SemaphoreType.DMA((4,))],
        compiler_params=pltpu.CompilerParams(vmem_limit_bytes=LIMIT),
        name="pack",
    )(strip_map, *flats, lateral_four)
    arrived = exchange(outgoing)
    folds = [fold_matrix(strip_map, plan, section) for section in range(3)]
    arrived, folds = lax.optimization_barrier((arrived, folds))

    half = owners // 2
    heights = [x // owners for x in (width, *channels[:2], c1)]
    chains = CHAINS
    tall = round_up(sum(heights), 8)
    cuts = [round_up(tall * c // chains, 8) for c in range(chains)] + [tall]
    chain_heights = [high - low for low, high in zip(cuts, cuts[1:])]
    early = (lateral_one, fine, join_weight, cot)
    straight, hidden_grad = pl.pallas_call(
        ahead_kernel,
        out_shape=(shape_of(total, width, dtype=F32),) * 2,
        in_specs=[ANY] * 4,
        out_specs=(ANY,) * 2,
        scratch_shapes=[pltpu.VMEM(x.shape, BF16) for x in early]
        + [pltpu.VMEM((total, width), F32)] * 2
        + [pltpu.SemaphoreType.DMA((4,)), pltpu.SemaphoreType.DMA((2,))],
        compiler_params=pltpu.CompilerParams(vmem_limit_bytes=LIMIT),
        cost_estimate=pl.CostEstimate(
            flops=4 * total * width * (width + c1), bytes_accessed=14_000_000, transcendentals=0
        ),
        name="ahead",
    )(*early)
    operands = (
        arrived,
        lateral_two,
        lateral_three,
        up,
        down,
        straight,
        hidden_grad,
        cot,
        fine,
        lateral_one,
    )
    stage = (shape_of(total, c1), shape_of(owners, plan.returned, LANES))
    stage += tuple(shape_of(half, height, width) for height in chain_heights) * 2
    grad_fine, back, *halves = pl.pallas_call(
        functools.partial(strip_kernel, plan, TURNS, chains),
        out_shape=stage,
        in_specs=[SMEM] + [ANY] * 10,
        out_specs=(ANY,) * len(stage),
        scratch_shapes=[pltpu.VMEM(x.shape, x.dtype) for x in operands + stage]
        + [
            pltpu.VMEM((owners * plan.per_owner, width), BF16),
            pltpu.VMEM((total, width), BF16),
            pltpu.VMEM((total, width), BF16),
        ]
        + [pltpu.VMEM((owners, count, width), BF16) for count in plan.counts]
        + [pltpu.VMEM((x, width), F32) for x in (width, *channels[:2], c1)]
        + [
            pltpu.SemaphoreType.DMA((len(stage),)),
            pltpu.SemaphoreType.DMA((8,)),
            pltpu.SemaphoreType.DMA((2, TURNS)),
        ],
        compiler_params=pltpu.CompilerParams(vmem_limit_bytes=LIMIT),
        cost_estimate=pl.CostEstimate(
            flops=4_000_000_000, bytes_accessed=16_000_000, transcendentals=total * width
        ),
        name="strip_work",
    )(core, *operands)

    levels = tuple(range(bits - 2, bits)), tuple(range(bits - 2))
    slices = jnp.take(arrived[:, plan.slice_at :], me ^ gather_pattern(levels), axis=0)
    grad_fine = jnp.transpose(grad_fine.reshape(fine_features.shape), (1, 2, 0))
    rest = [
        Halving(plus(keep, swap(give, 0)), range(1, bits))
        for keep, give in zip(halves[:chains], halves[chains:])
    ]
    halved = [chain.split() for chain in rest]
    halved = [(keep, swap(give, bit)) for keep, give, bit in halved]
    returned = exchange(back)
    returned, grad_fine, slices = lax.optimization_barrier((returned, grad_fine, slices))

    folded_four = pl.pallas_call(
        functools.partial(fold_kernel, plan),
        out_shape=shape_of(plan.coarse[2], width),
        in_specs=[VMEM] * 2,
        out_specs=VMEM,
        compiler_params=pltpu.CompilerParams(vmem_limit_bytes=8 * MEBI),
        name="fold_four",
    )(returned, folds[2])
    *halved, folded_four = lax.optimization_barrier((*halved, folded_four))
    for chain, (keep, received) in zip(rest, halved):
        chain.values = plus(keep, received)
    operands = (returned, *folds[:2], lateral_three, lateral_four, folded_four)
    grads = pl.pallas_call(
        functools.partial(section_kernel, plan),
        out_shape=tuple(shape_of(*f.shape) for f in flats),
        in_specs=[ANY] * 6,
        out_specs=(VMEM,) * 3,
        scratch_shapes=[pltpu.VMEM(x.shape, BF16) for x in operands] + [pltpu.SemaphoreType.DMA((6,))],
        compiler_params=pltpu.CompilerParams(vmem_limit_bytes=SMALL),
        cost_estimate=pl.CostEstimate(flops=500_000_000, bytes_accessed=6_000_000, transcendentals=0),
        name="section_grads",
    )(*operands)

    gathered = folded_four[None]
    for turn in range(bits - 2):
        if turn == 0:
            gathered = jnp.concatenate(gather_level(gathered, levels[0]))
            for chain in rest:
                chain.step()
        else:
            for chain in rest:
                gathered = chain.step(gathered)
        if turn < bits - 3:
            *values, grads, gathered = lax.optimization_barrier(
                (*[chain.values for chain in rest], grads, gathered)
            )
            for chain, value in zip(rest, values):
                chain.values = value
    gathered = gather_level(gathered, levels[1])

    operands = tuple(term for chain in rest for term in chain.terms)
    operands += (slices.reshape(-1, LANES), *[g.reshape(-1, width) for g in gathered])
    results = pl.pallas_call(
        functools.partial(finish_kernel, plan, chains),
        out_shape=(
            *[shape_of(height, width, dtype=F32) for height in heights],
            shape_of(plan.slice_width, width, dtype=F32),
        ),
        in_specs=[ANY] * len(operands),
        out_specs=(VMEM,) * 5,
        scratch_shapes=[pltpu.VMEM(x.shape, BF16) for x in operands]
        + [pltpu.SemaphoreType.DMA((len(operands),))],
        compiler_params=pltpu.CompilerParams(vmem_limit_bytes=LIMIT),
        name="finish",
    )(*operands)
    join_grad, two_grad, three_grad, one_grad, four_grad = results
    return (
        jnp.transpose(grad_fine, (2, 0, 1)),
        *[g.reshape(s.shape) for g, s in zip(grads, sections)],
        join_grad.T,
        one_grad,
        two_grad,
        three_grad,
        four_grad,
    )


def solution(mesh):
    fine_spec = P(None, ("group", "row"), None)
    coarse_spec = P("row", "group", None)
    weight_spec = P(("group", "row"), None)
    return jax.shard_map(
        body,
        mesh=mesh,
        in_specs=(fine_spec,) + (coarse_spec,) * 3 + (P("group"),) + (P(),) * 5 + (fine_spec,),
        out_specs=(fine_spec,) + (coarse_spec,) * 3 + (P("group", "row"),) + (weight_spec,) * 4,
        check_vma=False,
    )
```

```python
import functools

import jax
import jax.numpy as jnp
import numpy as np
from jax import lax
from jax.experimental import pallas as pl
from jax.experimental.pallas import tpu as pltpu
from jax.sharding import PartitionSpec as P

F32 = jnp.float32
BF16 = jnp.bfloat16
FACTORS = (2, 4, 8)
LANES = 128
VMEM = pl.BlockSpec(memory_space=pltpu.VMEM)
SMEM = pl.BlockSpec(memory_space=pltpu.SMEM)
ANY = pl.BlockSpec(memory_space=pl.ANY)
MEBI = 1024 * 1024
LIMIT = 62 * MEBI
SMALL = 62 * MEBI
STRIP = 58 * MEBI
TURNS = 4
CHAINS = 1


def round_up(value, multiple):
    return -(-value // multiple) * multiple


class Plan:
    def __init__(self, owners, depth, strip_width, channels, width):
        self.owners, self.depth, self.strip_width = owners, depth, strip_width
        self.channels, self.width = channels, width
        self.rows = [depth * 8 // k for k in FACTORS]
        self.columns = [strip_width // k for k in FACTORS]
        self.coarse = [r * c * owners for r, c in zip(self.rows, self.columns)]
        self.entries, self.counts, self.starts = [], [], []
        at = 0
        for rows, columns in zip(self.rows, self.columns):
            entries = [(r, c) for r in range(rows) for c in range(columns + 2)]
            entries += [None] * (-len(entries) % 8)
            self.entries.append(entries)
            self.counts.append(len(entries))
            self.starts.append(at)
            at += len(entries)
        self.per_owner = round_up(at, 16)
        self.out_at, self.back_at = [], []
        self.sent = self.returned = 0
        for section in range(3):
            self.out_at.append(self.sent)
            self.sent += self.counts[section] * (self.out_width(section) // LANES)
        for section in range(3):
            self.back_at.append(self.returned)
            self.returned += self.counts[section] * (self.back_width(section) // LANES)
        self.slice_at = self.sent
        self.slice_width = channels[2] // owners
        self.sent += self.coarse[2]

    def out_width(self, section):
        return self.channels[section] if section < 2 else self.width

    def back_width(self, section):
        return self.channels[0] if section == 0 else self.width


def axis_weights(fine_count, factor):
    matrix = np.zeros((fine_count, fine_count // factor + 2), np.float32)
    for fine in range(fine_count):
        base, phase = divmod(fine, factor)
        offset = (phase + 0.5) / factor - 0.5
        if offset < 0:
            matrix[fine, base] += -offset
            matrix[fine, base + 1] += 1.0 + offset
        else:
            matrix[fine, base + 1] += 1.0 - offset
            matrix[fine, base + 2] += offset
    return matrix


def clamp_rows(matrix):
    folded = matrix[:, 1:-1].copy()
    folded[:, 0] += matrix[:, 0]
    folded[:, -1] += matrix[:, -1]
    return folded


def window_matrices(plan):
    owners, strip_width = plan.owners, plan.strip_width
    block_rows = plan.depth * 8
    fine_rows = owners * block_rows
    whole = np.zeros((fine_rows, strip_width, owners, plan.per_owner), np.float32)
    row_mats = [clamp_rows(axis_weights(fine_rows, k)) for k in FACTORS]
    col_mats = [axis_weights(strip_width, k) for k in FACTORS]
    for owner in range(owners):
        for section in range(3):
            for index, entry in enumerate(plan.entries[section]):
                if entry is not None:
                    at = owner * plan.rows[section] + entry[0]
                    whole[:, :, owner, plan.starts[section] + index] = np.outer(
                        row_mats[section][:, at], col_mats[section][:, entry[1]]
                    )
    up, down = [], []
    for owner in (0, 1, owners - 1):
        start = min(max(owner - 1, 0), owners - 3)
        rows = slice(owner * block_rows, (owner + 1) * block_rows)
        up.append(
            whole[rows, :, start : start + 3].reshape(block_rows * strip_width, 3 * plan.per_owner)
        )
        window = block_rows + 8
        low = min(max(owner * block_rows - 4, 0), fine_rows - window)
        piece = whole[low : low + window, :, owner]
        down.append(piece.reshape(window * strip_width, plan.per_owner).T)
    return np.stack(up).astype(BF16), np.stack(down).astype(BF16)


def entry_tables(plan, section):
    entries, columns = plan.entries[section], plan.columns[section]
    start = [-(1 << 20) if e is None else e[0] * columns * plan.owners for e in entries]
    offset = [0 if e is None else e[1] - 1 for e in entries]
    return np.array(start, np.int32), np.array(offset, np.int32)


def fold_matrix(strip_map, plan, section):
    start, offset = entry_tables(plan, section)
    columns = plan.columns[section]
    column = jnp.clip(strip_map[:, None] * columns + offset, 0, plan.owners * columns - 1)
    target = (column + start).reshape(-1)
    places = np.arange(plan.coarse[section], dtype=np.int32)
    return (places[:, None] == target[None]).astype(BF16)


def contract(left, right, left_dim, right_dim):
    return lax.dot_general(
        left, right, (((left_dim,), (right_dim,)), ((), ())), preferred_element_type=F32
    )


def put_pieces(ref, at, values, count):
    owners = ref.shape[0]
    for piece in range(values.shape[1] // LANES):
        part = values[:, piece * LANES : (piece + 1) * LANES]
        ref[:, at + piece * count : at + (piece + 1) * count, :] = part.reshape(owners, count, LANES)


def take_pieces(ref, at, pieces, count):
    owners = ref.shape[0]
    return jnp.concatenate(
        [
            ref[:, at + p * count : at + (p + 1) * count, :].reshape(owners * count, LANES)
            for p in range(pieces)
        ],
        axis=1,
    )


def copies_in(pairs, sem_ref):
    copies = [pltpu.make_async_copy(src, dst, sem_ref.at[i]) for i, (src, dst) in enumerate(pairs)]
    for copy in copies:
        copy.start()
    return copies


def entry_vectors(plan, section, shape):
    entry = lax.broadcasted_iota(jnp.int32, shape, 0)
    columns = plan.columns[section]
    span = columns + 2
    scale = -(-65536 // span)
    assert all((q * scale) >> 16 == q // span for q in range(shape[0]))
    row = (entry * scale) >> 16
    start = jnp.where(row < plan.rows[section], row * (columns * plan.owners), -(1 << 20))
    return start, entry - row * span - 1


def pack_kernel(plan, map_ref, *refs):
    sources, out_ref = refs[:4], refs[4]
    held, picks, sem_ref = refs[5:9], refs[9:12], refs[12]
    copies = copies_in(list(zip(sources, held)), sem_ref)
    four_ref, l4_ref = held[2:]
    for section in range(3):
        columns, count, places = plan.columns[section], plan.counts[section], plan.coarse[section]
        start, offset = entry_vectors(plan, section, (count, min(LANES, places)))
        lane = lax.broadcasted_iota(jnp.int32, start.shape, 1) - start
        for device in range(plan.owners):
            column = jnp.clip(map_ref[device] * columns + offset, 0, plan.owners * columns - 1)
            ahead = lane - column
            for at in range(0, places, LANES):
                picks[section][device, :, at : at + LANES] = jnp.where(ahead == -at, 1.0, 0.0).astype(BF16)
    for section in range(3):
        count = plan.counts[section]
        pick = picks[section][...].reshape(plan.owners * count, plan.coarse[section])
        copies[section].wait()
        values = held[section][...]
        if section == 2:
            copies[3].wait()
            values = contract(values, l4_ref[...], 1, 0).astype(BF16)
        put_pieces(out_ref, plan.out_at[section], contract(pick, values, 1, 0).astype(BF16), count)
    count = plan.coarse[2]
    fill = jnp.zeros((count, LANES - plan.slice_width), BF16)
    for owner in range(plan.owners):
        part = four_ref[:, owner * plan.slice_width : (owner + 1) * plan.slice_width]
        out_ref[owner, plan.slice_at :, :] = jnp.concatenate([part, fill], axis=1)


def put_parts(part_refs, even_refs, odd_refs):
    owners = 2 * even_refs[0].shape[0]
    for owner in range(owners):
        refs = (even_refs, odd_refs)[owner % 2]
        index, at = 0, 0
        for part_ref in part_refs:
            height = part_ref.shape[0] // owners
            done = 0
            while done < height:
                if at == refs[index].shape[1]:
                    index, at = index + 1, 0
                count = min(height - done, refs[index].shape[1] - at)
                first = owner * height + done
                refs[index][owner // 2, at : at + count, :] = part_ref[first : first + count, :].astype(BF16)
                done += count
                at += count
        if at < refs[index].shape[1]:
            fill = jnp.zeros((refs[index].shape[1] - at, refs[index].shape[2]), BF16)
            refs[index][owner // 2, at:, :] = fill


def ahead_kernel(*refs):
    sources, outs = refs[:4], refs[4:6]
    held, stage, in_sem, out_sem = refs[6:10], refs[10:12], refs[12], refs[13]
    l1_ref, fine_ref, join_ref, cot_ref = held
    copies = copies_in(list(zip(sources, held)), in_sem)
    copies[0].wait()
    copies[1].wait()
    stage[0][...] = contract(fine_ref[...], l1_ref[...], 1, 0).astype(BF16)
    first = pltpu.make_async_copy(stage[0], outs[0], out_sem.at[0])
    first.start()
    copies[2].wait()
    copies[3].wait()
    stage[1][...] = contract(cot_ref[...], join_ref[...], 1, 1).astype(BF16)
    second = pltpu.make_async_copy(stage[1], outs[1], out_sem.at[1])
    second.start()
    first.wait()
    second.wait()


def take_features(plan, arrived_ref, section):
    return take_pieces(
        arrived_ref, plan.out_at[section], plan.out_width(section) // LANES, plan.counts[section]
    )


def strip_kernel(plan, turns, chains, core_ref, *refs):
    sent = 2 + 2 * chains
    arrived_ref, sources, outs = refs[0], refs[1:10], refs[10 : 10 + sent]
    held, stage, refs = refs[10 + sent : 19 + sent], refs[19 + sent : 19 + 2 * sent], refs[19 + 2 * sent :]
    l2_ref, l3_ref, up_ref, down_ref, straight_ref, hidden_grad_ref, cot_ref, fine_ref, l1_ref = held
    grad_fine_ref, back_ref = stage[:2]
    coarse_ref, hidden_ref, joined_grad_ref = refs[:3]
    grad_refs = refs[3:6]
    join_part_ref, two_part_ref, three_part_ref, one_part_ref, out_sem, in_sem, turn_sem = refs[6:]
    owners, per_owner, width = plan.owners, plan.per_owner, plan.width
    core = core_ref[0]
    block = up_ref.shape[1]
    reach = up_ref.shape[2]
    window = down_ref.shape[2]
    total = cot_ref.shape[0]
    group = owners // turns
    copies = copies_in(list(zip(sources[:4], held[:4])), in_sem)
    turn_copies = []
    for turn in range(turns):
        many = pl.ds(turn * group * block, group * block)
        for which in (0, 1):
            copy = pltpu.make_async_copy(
                sources[4 + which].at[many], held[4 + which].at[many], turn_sem.at[which, turn]
            )
            copy.start()
            turn_copies.append(copy)
    late_copies = []
    for index in (6, 7, 8):
        copy = pltpu.make_async_copy(sources[index], held[index], in_sem.at[index - 2])
        copy.start()
        late_copies.append(copy)

    def leave(index):
        copy = pltpu.make_async_copy(stage[index], outs[index], out_sem.at[index])
        copy.start()
        return copy

    features = [
        take_pieces(arrived_ref, plan.out_at[section], plan.out_width(section) // LANES, plan.counts[section])
        for section in range(3)
    ]
    projected = []
    for section in range(3):
        product = features[section]
        if section < 2:
            copies[section].wait()
            product = contract(product, (l2_ref, l3_ref)[section][...], 1, 0).astype(BF16)
        projected.append(product.reshape(owners, plan.counts[section], width))
    tail = per_owner - sum(plan.counts)
    if tail:
        projected.append(jnp.zeros((owners, tail, width), BF16))
    coarse_ref[...] = jnp.concatenate(projected, axis=1).reshape(owners * per_owner, width)
    copies[2].wait()
    copies[3].wait()

    for turn in range(turns):
        turn_copies[2 * turn].wait()
        turn_copies[2 * turn + 1].wait()
        for owner in range(turn * group, (turn + 1) * group):
            kind = 0 if owner == 0 else 2 if owner == owners - 1 else 1
            start = min(max(owner - 1, 0), owners - 3) * per_owner
            rows = slice(owner * block, (owner + 1) * block)
            joined = straight_ref[rows, :].astype(F32) + contract(
                up_ref[kind], coarse_ref[start : start + reach, :], 1, 0
            )
            gate = 0.5 + 0.5 * jnp.tanh(0.5 * joined)
            hidden = joined * gate
            hidden_ref[rows, :] = hidden.astype(BF16)
            slope = gate + hidden * (1.0 - gate)
            joined_grad_ref[rows, :] = (hidden_grad_ref[rows, :].astype(F32) * slope).astype(BF16)

    for owner in range(owners):
        kind = 0 if owner == 0 else 2 if owner == owners - 1 else 1
        low = min(max(owner * block - 32, 0), total - window)
        strip_grad = contract(down_ref[kind], joined_grad_ref[low : low + window, :], 1, 0)
        for section, ref in enumerate(grad_refs):
            at = plan.starts[section]
            ref[owner] = strip_grad[at : at + plan.counts[section]].astype(BF16)
    strip_grads = [ref[...].reshape(owners * count, width) for ref, count in zip(grad_refs, plan.counts)]
    for section in (1, 2):
        put_pieces(back_ref, plan.back_at[section], strip_grads[section], plan.counts[section])
    put_pieces(back_ref, 0, contract(strip_grads[0], l2_ref[...], 1, 1).astype(BF16), plan.counts[0])
    leaving = [leave(1)]
    two_part_ref[...] = contract(features[0], strip_grads[0], 0, 0)
    three_part_ref[...] = contract(features[1], strip_grads[1], 0, 0)
    for copy in late_copies:
        copy.wait()
    join_part_ref[...] = contract(cot_ref[...], hidden_ref[...], 0, 0)
    one_part_ref[...] = contract(fine_ref[...], joined_grad_ref[...], 0, 0)
    kept, given = stage[2 : 2 + chains], stage[2 + chains :]
    parts = (join_part_ref, two_part_ref, three_part_ref, one_part_ref)

    @pl.when(core == 0)
    def _():
        put_parts(parts, kept, given)

    @pl.when(core != 0)
    def _():
        put_parts(parts, given, kept)

    leaving += [leave(index) for index in range(2, sent)]
    grad_fine_ref[...] = contract(joined_grad_ref[...], l1_ref[...], 1, 1).astype(BF16)
    leaving.append(leave(0))
    for copy in leaving:
        copy.wait()


def finish_kernel(plan, chains, *refs):
    sums, (slices_ref, *pieces), outs = refs[:chains], refs[chains:-5], refs[-5:]
    total = jnp.concatenate([ref[...] for ref in sums])
    join_ref, two_ref, three_ref, one_ref, four_ref = outs
    at = 0
    for ref in (join_ref, two_ref, three_ref, one_ref):
        ref[...] = total[at : at + ref.shape[0]]
        at += ref.shape[0]
    blocks = jnp.concatenate([piece[...] for piece in pieces])
    four_ref[...] = contract(slices_ref[...], blocks, 0, 0)[: four_ref.shape[0]]


def fold_kernel(plan, returned_ref, fold_ref, out_ref):
    arrived = take_pieces(returned_ref, plan.back_at[2], plan.back_width(2) // LANES, plan.counts[2])
    out_ref[...] = contract(fold_ref[...], arrived, 1, 0).astype(BF16)


def section_kernel(plan, *refs):
    sources, outs, held, sem_ref = refs[:6], refs[6:9], refs[9:15], refs[15]
    copies = copies_in(list(zip(sources, held)), sem_ref)
    returned_ref, folds, l3_ref, l4_ref, four_ref = held[0], held[1:3], held[3], held[4], held[5]
    copies[0].wait()
    for section in range(2):
        arrived = take_pieces(
            returned_ref, plan.back_at[section], plan.back_width(section) // LANES, plan.counts[section]
        )
        copies[1 + section].wait()
        folded = contract(folds[section][...], arrived, 1, 0).astype(BF16)
        if section == 1:
            copies[3].wait()
            folded = contract(folded, l3_ref[...], 1, 1).astype(BF16)
        outs[section][...] = folded
    copies[4].wait()
    copies[5].wait()
    outs[2][...] = contract(four_ref[...], l4_ref[...], 1, 1).astype(BF16)


def swap(values, bit):
    owners = lax.axis_size("row")
    return lax.ppermute(values, "row", [(i, i ^ (1 << bit)) for i in range(owners)])


def plus(left, right):
    return (left.astype(F32) + right.astype(F32)).astype(BF16)


class Halving:
    def __init__(self, values, order):
        bits = len(order)
        self.values = values.reshape((2,) * bits + values.shape[1:])
        self.left = sorted(order, reverse=True)
        self.order = list(order)

    def split(self):
        bit = self.order.pop(0)
        axis = self.left.index(bit)
        self.left.pop(axis)
        mine = (lax.axis_index("row") >> bit) & 1
        keep = lax.dynamic_index_in_dim(self.values, mine, axis, keepdims=False)
        give = lax.dynamic_index_in_dim(self.values, 1 - mine, axis, keepdims=False)
        return keep, give, bit

    def step(self, later=None):
        keep, give, bit = self.split()
        if later is not None:
            give, later = lax.optimization_barrier((give, later))
        if self.order:
            self.values = plus(keep, swap(give, bit))
        else:
            self.terms = keep, swap(give, bit)
        return later


def level_swaps(level):
    distances = [0]
    for bit in level:
        distances += [d ^ (1 << bit) for d in distances]
    return distances


def gather_level(stacked, level):
    owners = lax.axis_size("row")
    distances = level_swaps(level)[1:]
    return [stacked] + [lax.ppermute(stacked, "row", [(i, i ^ d) for i in range(owners)]) for d in distances]


def gather_pattern(levels):
    pattern = np.zeros((1,), np.int32)
    for level in levels:
        pattern = np.concatenate([pattern ^ d for d in level_swaps(level)])
    return pattern


def shape_of(*dims, dtype=BF16):
    return jax.ShapeDtypeStruct(dims, dtype)


def body(
    fine_features,
    section_two,
    section_three,
    section_four,
    strip_map,
    lateral_one,
    lateral_two,
    lateral_three,
    lateral_four,
    join_weight,
    cotangent,
):
    owners = lax.axis_size("row")
    bits = owners.bit_length() - 1
    fine_height, strip_width, c1 = fine_features.shape
    width = join_weight.shape[0]
    sections = (section_two, section_three, section_four)
    channels = [s.shape[-1] for s in sections]
    plan = Plan(owners, section_four.shape[0], strip_width, channels, width)
    flats = [s.reshape(-1, s.shape[-1]) for s in sections]
    fine = fine_features.reshape(-1, c1)
    cot = cotangent.reshape(-1, width)
    total = fine.shape[0]
    me = lax.axis_index("row")
    core = (me & 1).astype(jnp.int32).reshape(1)
    up, down = window_matrices(plan)
    exchange = functools.partial(lax.all_to_all, axis_name="row", split_axis=0, concat_axis=0, tiled=True)

    outgoing = pl.pallas_call(
        functools.partial(pack_kernel, plan),
        out_shape=shape_of(owners, plan.sent, LANES),
        in_specs=[SMEM] + [ANY] * 4,
        out_specs=VMEM,
        scratch_shapes=[pltpu.VMEM(x.shape, BF16) for x in (*flats, lateral_four)]
        + [pltpu.VMEM((owners, count, places), BF16) for count, places in zip(plan.counts, plan.coarse)]
        + [pltpu.SemaphoreType.DMA((4,))],
        compiler_params=pltpu.CompilerParams(vmem_limit_bytes=LIMIT),
        name="pack",
    )(strip_map, *flats, lateral_four)
    arrived = exchange(outgoing)
    folds = [fold_matrix(strip_map, plan, section) for section in range(3)]
    arrived, folds = lax.optimization_barrier((arrived, folds))

    half = owners // 2
    heights = [x // owners for x in (width, *channels[:2], c1)]
    chains = CHAINS
    tall = round_up(sum(heights), 8)
    cuts = [round_up(tall * c // chains, 8) for c in range(chains)] + [tall]
    chain_heights = [high - low for low, high in zip(cuts, cuts[1:])]
    early = (lateral_one, fine, join_weight, cot)
    straight, hidden_grad = pl.pallas_call(
        ahead_kernel,
        out_shape=(shape_of(total, width),) * 2,
        in_specs=[ANY] * 4,
        out_specs=(ANY,) * 2,
        scratch_shapes=[pltpu.VMEM(x.shape, BF16) for x in early]
        + [pltpu.VMEM((total, width), BF16)] * 2
        + [pltpu.SemaphoreType.DMA((4,)), pltpu.SemaphoreType.DMA((2,))],
        compiler_params=pltpu.CompilerParams(vmem_limit_bytes=LIMIT),
        cost_estimate=pl.CostEstimate(
            flops=4 * total * width * (width + c1), bytes_accessed=8_000_000, transcendentals=0
        ),
        name="ahead",
    )(*early)
    operands = (
        arrived,
        lateral_two,
        lateral_three,
        up,
        down,
        straight,
        hidden_grad,
        cot,
        fine,
        lateral_one,
    )
    stage = (shape_of(total, c1), shape_of(owners, plan.returned, LANES))
    stage += tuple(shape_of(half, height, width) for height in chain_heights) * 2
    grad_fine, back, *halves = pl.pallas_call(
        functools.partial(strip_kernel, plan, TURNS, chains),
        out_shape=stage,
        in_specs=[SMEM, VMEM] + [ANY] * 9,
        out_specs=(ANY,) * len(stage),
        scratch_shapes=[pltpu.VMEM(x.shape, x.dtype) for x in operands[1:] + stage]
        + [
            pltpu.VMEM((owners * plan.per_owner, width), BF16),
            pltpu.VMEM((total, width), BF16),
            pltpu.VMEM((total, width), BF16),
        ]
        + [pltpu.VMEM((owners, count, width), BF16) for count in plan.counts]
        + [pltpu.VMEM((x, width), F32) for x in (width, *channels[:2], c1)]
        + [
            pltpu.SemaphoreType.DMA((len(stage),)),
            pltpu.SemaphoreType.DMA((7,)),
            pltpu.SemaphoreType.DMA((2, TURNS)),
        ],
        compiler_params=pltpu.CompilerParams(vmem_limit_bytes=STRIP),
        cost_estimate=pl.CostEstimate(
            flops=4_000_000_000, bytes_accessed=16_000_000, transcendentals=total * width
        ),
        name="strip_work",
    )(core, *operands)

    levels = tuple(range(bits - 2, bits)), tuple(range(bits - 2))
    slices = jnp.take(arrived[:, plan.slice_at :], me ^ gather_pattern(levels), axis=0)
    grad_fine = jnp.transpose(grad_fine.reshape(fine_features.shape), (1, 2, 0))
    rest = [
        Halving(plus(keep, swap(give, 0)), range(1, bits))
        for keep, give in zip(halves[:chains], halves[chains:])
    ]
    halved = [chain.split() for chain in rest]
    halved = [(keep, swap(give, bit)) for keep, give, bit in halved]
    returned = exchange(back)
    returned, grad_fine, slices = lax.optimization_barrier((returned, grad_fine, slices))

    folded_four = pl.pallas_call(
        functools.partial(fold_kernel, plan),
        out_shape=shape_of(plan.coarse[2], width),
        in_specs=[VMEM] * 2,
        out_specs=VMEM,
        compiler_params=pltpu.CompilerParams(vmem_limit_bytes=8 * MEBI),
        name="fold_four",
    )(returned, folds[2])
    *halved, folded_four = lax.optimization_barrier((*halved, folded_four))
    for chain, (keep, received) in zip(rest, halved):
        chain.values = plus(keep, received)
    operands = (returned, *folds[:2], lateral_three, lateral_four, folded_four)
    grads = pl.pallas_call(
        functools.partial(section_kernel, plan),
        out_shape=tuple(shape_of(*f.shape) for f in flats),
        in_specs=[ANY] * 6,
        out_specs=(VMEM,) * 3,
        scratch_shapes=[pltpu.VMEM(x.shape, BF16) for x in operands] + [pltpu.SemaphoreType.DMA((6,))],
        compiler_params=pltpu.CompilerParams(vmem_limit_bytes=SMALL),
        cost_estimate=pl.CostEstimate(flops=500_000_000, bytes_accessed=6_000_000, transcendentals=0),
        name="section_grads",
    )(*operands)

    gathered = folded_four[None]
    for turn in range(bits - 2):
        if turn == 0:
            gathered = jnp.concatenate(gather_level(gathered, levels[0]))
            for chain in rest:
                chain.step()
        else:
            for chain in rest:
                gathered = chain.step(gathered)
        if turn < bits - 3:
            *values, grads, gathered = lax.optimization_barrier(
                (*[chain.values for chain in rest], grads, gathered)
            )
            for chain, value in zip(rest, values):
                chain.values = value
    gathered = gather_level(gathered, levels[1])

    sums = [keep.astype(F32) + received.astype(F32) for keep, received in (chain.terms for chain in rest)]
    *sums, gathered = lax.optimization_barrier((*sums, gathered))
    operands = tuple(sums)
    operands += (slices.reshape(-1, LANES), *[g.reshape(-1, width) for g in gathered])
    results = pl.pallas_call(
        functools.partial(finish_kernel, plan, chains),
        out_shape=(
            *[shape_of(height, width, dtype=F32) for height in heights],
            shape_of(plan.slice_width, width, dtype=F32),
        ),
        in_specs=[VMEM] * len(operands),
        out_specs=(VMEM,) * 5,
        compiler_params=pltpu.CompilerParams(vmem_limit_bytes=16 * MEBI),
        name="finish",
    )(*operands)
    join_grad, two_grad, three_grad, one_grad, four_grad = results
    return (
        jnp.transpose(grad_fine, (2, 0, 1)),
        *[g.reshape(s.shape) for g, s in zip(grads, sections)],
        join_grad.T,
        one_grad,
        two_grad,
        three_grad,
        four_grad,
    )


def solution(mesh):
    fine_spec = P(None, ("group", "row"), None)
    coarse_spec = P("row", "group", None)
    weight_spec = P(("group", "row"), None)
    return jax.shard_map(
        body,
        mesh=mesh,
        in_specs=(fine_spec,) + (coarse_spec,) * 3 + (P("group"),) + (P(),) * 5 + (fine_spec,),
        out_specs=(fine_spec,) + (coarse_spec,) * 3 + (P("group", "row"),) + (weight_spec,) * 4,
        check_vma=False,
    )
```

```python
import functools

import jax
import jax.numpy as jnp
import numpy as np
from jax import lax
from jax.experimental import pallas as pl
from jax.experimental.pallas import tpu as pltpu
from jax.sharding import PartitionSpec as P

F32 = jnp.float32
BF16 = jnp.bfloat16
FACTORS = (2, 4, 8)
LANES = 128
VMEM = pl.BlockSpec(memory_space=pltpu.VMEM)
SMEM = pl.BlockSpec(memory_space=pltpu.SMEM)
ANY = pl.BlockSpec(memory_space=pl.ANY)
MEBI = 1024 * 1024
LIMIT = 62 * MEBI
SMALL = 62 * MEBI
STRIP = 58 * MEBI
TURNS = 4
CHAINS = 1


def round_up(value, multiple):
    return -(-value // multiple) * multiple


class Plan:
    def __init__(self, owners, depth, strip_width, channels, width):
        self.owners, self.depth, self.strip_width = owners, depth, strip_width
        self.channels, self.width = channels, width
        self.rows = [depth * 8 // k for k in FACTORS]
        self.columns = [strip_width // k for k in FACTORS]
        self.coarse = [r * c * owners for r, c in zip(self.rows, self.columns)]
        self.entries, self.counts, self.starts = [], [], []
        at = 0
        for rows, columns in zip(self.rows, self.columns):
            entries = [(r, c) for r in range(rows) for c in range(columns + 2)]
            entries += [None] * (-len(entries) % 8)
            self.entries.append(entries)
            self.counts.append(len(entries))
            self.starts.append(at)
            at += len(entries)
        self.per_owner = round_up(at, 16)
        self.out_at, self.back_at = [], []
        self.sent = self.returned = 0
        for section in range(3):
            self.out_at.append(self.sent)
            self.sent += self.counts[section] * (self.out_width(section) // LANES)
        for section in range(3):
            self.back_at.append(self.returned)
            self.returned += self.counts[section] * (self.back_width(section) // LANES)
        self.slice_at = self.sent
        self.slice_width = channels[2] // owners
        self.sent += self.coarse[2]

    def out_width(self, section):
        return self.channels[section] if section < 2 else self.width

    def back_width(self, section):
        return self.channels[0] if section == 0 else self.width


def axis_weights(fine_count, factor):
    matrix = np.zeros((fine_count, fine_count // factor + 2), np.float32)
    for fine in range(fine_count):
        base, phase = divmod(fine, factor)
        offset = (phase + 0.5) / factor - 0.5
        if offset < 0:
            matrix[fine, base] += -offset
            matrix[fine, base + 1] += 1.0 + offset
        else:
            matrix[fine, base + 1] += 1.0 - offset
            matrix[fine, base + 2] += offset
    return matrix


def clamp_rows(matrix):
    folded = matrix[:, 1:-1].copy()
    folded[:, 0] += matrix[:, 0]
    folded[:, -1] += matrix[:, -1]
    return folded


def window_matrices(plan):
    owners, strip_width = plan.owners, plan.strip_width
    block_rows = plan.depth * 8
    fine_rows = owners * block_rows
    whole = np.zeros((fine_rows, strip_width, owners, plan.per_owner), np.float32)
    row_mats = [clamp_rows(axis_weights(fine_rows, k)) for k in FACTORS]
    col_mats = [axis_weights(strip_width, k) for k in FACTORS]
    for owner in range(owners):
        for section in range(3):
            for index, entry in enumerate(plan.entries[section]):
                if entry is not None:
                    at = owner * plan.rows[section] + entry[0]
                    whole[:, :, owner, plan.starts[section] + index] = np.outer(
                        row_mats[section][:, at], col_mats[section][:, entry[1]]
                    )
    up, down = [], []
    for owner in (0, 1, owners - 1):
        start = min(max(owner - 1, 0), owners - 3)
        rows = slice(owner * block_rows, (owner + 1) * block_rows)
        up.append(
            whole[rows, :, start : start + 3].reshape(block_rows * strip_width, 3 * plan.per_owner)
        )
        window = block_rows + 8
        low = min(max(owner * block_rows - 4, 0), fine_rows - window)
        piece = whole[low : low + window, :, owner]
        down.append(piece.reshape(window * strip_width, plan.per_owner).T)
    return np.stack(up).astype(BF16), np.stack(down).astype(BF16)


def entry_tables(plan, section):
    entries, columns = plan.entries[section], plan.columns[section]
    start = [-(1 << 20) if e is None else e[0] * columns * plan.owners for e in entries]
    offset = [0 if e is None else e[1] - 1 for e in entries]
    return np.array(start, np.int32), np.array(offset, np.int32)


def fold_matrix(strip_map, plan, section):
    start, offset = entry_tables(plan, section)
    columns = plan.columns[section]
    column = jnp.clip(strip_map[:, None] * columns + offset, 0, plan.owners * columns - 1)
    target = (column + start).reshape(-1)
    places = np.arange(plan.coarse[section], dtype=np.int32)
    return (places[:, None] == target[None]).astype(BF16)


def contract(left, right, left_dim, right_dim):
    return lax.dot_general(
        left, right, (((left_dim,), (right_dim,)), ((), ())), preferred_element_type=F32
    )


def put_pieces(ref, at, values, count):
    owners = ref.shape[0]
    for piece in range(values.shape[1] // LANES):
        part = values[:, piece * LANES : (piece + 1) * LANES]
        ref[:, at + piece * count : at + (piece + 1) * count, :] = part.reshape(owners, count, LANES)


def take_pieces(ref, at, pieces, count):
    owners = ref.shape[0]
    return jnp.concatenate(
        [
            ref[:, at + p * count : at + (p + 1) * count, :].reshape(owners * count, LANES)
            for p in range(pieces)
        ],
        axis=1,
    )


def copies_in(pairs, sem_ref):
    copies = [pltpu.make_async_copy(src, dst, sem_ref.at[i]) for i, (src, dst) in enumerate(pairs)]
    for copy in copies:
        copy.start()
    return copies


def entry_vectors(plan, section, shape):
    entry = lax.broadcasted_iota(jnp.int32, shape, 0)
    columns = plan.columns[section]
    span = columns + 2
    scale = -(-65536 // span)
    assert all((q * scale) >> 16 == q // span for q in range(shape[0]))
    row = (entry * scale) >> 16
    start = jnp.where(row < plan.rows[section], row * (columns * plan.owners), -(1 << 20))
    return start, entry - row * span - 1


def pack_kernel(plan, map_ref, *refs):
    sources, out_ref = refs[:4], refs[4]
    held, picks, sem_ref = refs[5:9], refs[9:12], refs[12]
    copies = copies_in(list(zip(sources, held)), sem_ref)
    four_ref, l4_ref = held[2:]
    for section in range(3):
        columns, count, places = plan.columns[section], plan.counts[section], plan.coarse[section]
        start, offset = entry_vectors(plan, section, (count, min(LANES, places)))
        lane = lax.broadcasted_iota(jnp.int32, start.shape, 1) - start
        for device in range(plan.owners):
            column = jnp.clip(map_ref[device] * columns + offset, 0, plan.owners * columns - 1)
            ahead = lane - column
            for at in range(0, places, LANES):
                picks[section][device, :, at : at + LANES] = jnp.where(ahead == -at, 1.0, 0.0).astype(BF16)
    for section in range(3):
        count = plan.counts[section]
        pick = picks[section][...].reshape(plan.owners * count, plan.coarse[section])
        copies[section].wait()
        values = held[section][...]
        if section == 2:
            copies[3].wait()
            values = contract(values, l4_ref[...], 1, 0).astype(BF16)
        put_pieces(out_ref, plan.out_at[section], contract(pick, values, 1, 0).astype(BF16), count)
    count = plan.coarse[2]
    fill = jnp.zeros((count, LANES - plan.slice_width), BF16)
    for owner in range(plan.owners):
        part = four_ref[:, owner * plan.slice_width : (owner + 1) * plan.slice_width]
        out_ref[owner, plan.slice_at :, :] = jnp.concatenate([part, fill], axis=1)


def put_parts(part_refs, even_refs, odd_refs):
    owners = 2 * even_refs[0].shape[0]
    for owner in range(owners):
        refs = (even_refs, odd_refs)[owner % 2]
        index, at = 0, 0
        for part_ref in part_refs:
            height = part_ref.shape[0] // owners
            done = 0
            while done < height:
                if at == refs[index].shape[1]:
                    index, at = index + 1, 0
                count = min(height - done, refs[index].shape[1] - at)
                first = owner * height + done
                refs[index][owner // 2, at : at + count, :] = part_ref[first : first + count, :].astype(BF16)
                done += count
                at += count
        if at < refs[index].shape[1]:
            fill = jnp.zeros((refs[index].shape[1] - at, refs[index].shape[2]), BF16)
            refs[index][owner // 2, at:, :] = fill


def ahead_kernel(*refs):
    sources, outs = refs[:4], refs[4:6]
    held, stage, in_sem, out_sem = refs[6:10], refs[10:12], refs[12], refs[13]
    l1_ref, fine_ref, join_ref, cot_ref = held
    copies = copies_in(list(zip(sources, held)), in_sem)
    copies[0].wait()
    copies[1].wait()
    stage[0][...] = contract(fine_ref[...], l1_ref[...], 1, 0).astype(BF16)
    first = pltpu.make_async_copy(stage[0], outs[0], out_sem.at[0])
    first.start()
    copies[2].wait()
    copies[3].wait()
    stage[1][...] = contract(cot_ref[...], join_ref[...], 1, 1).astype(BF16)
    second = pltpu.make_async_copy(stage[1], outs[1], out_sem.at[1])
    second.start()
    first.wait()
    second.wait()


def take_features(plan, arrived_ref, section):
    return take_pieces(
        arrived_ref, plan.out_at[section], plan.out_width(section) // LANES, plan.counts[section]
    )


def strip_kernel(plan, turns, chains, core_ref, *refs):
    sent = 2 + 2 * chains
    arrived_ref, sources, outs = refs[0], refs[1:10], refs[10 : 10 + sent]
    held, stage, refs = refs[10 + sent : 19 + sent], refs[19 + sent : 19 + 2 * sent], refs[19 + 2 * sent :]
    l2_ref, l3_ref, up_ref, down_ref, straight_ref, hidden_grad_ref, cot_ref, fine_ref, l1_ref = held
    grad_fine_ref, back_ref = stage[:2]
    coarse_ref, hidden_ref, joined_grad_ref = refs[:3]
    grad_refs = refs[3:6]
    join_part_ref, two_part_ref, three_part_ref, one_part_ref, out_sem, in_sem, turn_sem = refs[6:]
    owners, per_owner, width = plan.owners, plan.per_owner, plan.width
    core = core_ref[0]
    block = up_ref.shape[1]
    reach = up_ref.shape[2]
    window = down_ref.shape[2]
    total = cot_ref.shape[0]
    group = owners // turns
    copies = copies_in(list(zip(sources[:4], held[:4])), in_sem)
    turn_copies = []
    for turn in range(turns):
        many = pl.ds(turn * group * block, group * block)
        for which in (0, 1):
            copy = pltpu.make_async_copy(
                sources[4 + which].at[many], held[4 + which].at[many], turn_sem.at[which, turn]
            )
            copy.start()
            turn_copies.append(copy)
    late_copies = []
    for index in (6, 7, 8):
        copy = pltpu.make_async_copy(sources[index], held[index], in_sem.at[index - 2])
        copy.start()
        late_copies.append(copy)

    def leave(index):
        copy = pltpu.make_async_copy(stage[index], outs[index], out_sem.at[index])
        copy.start()
        return copy

    features = [
        take_pieces(arrived_ref, plan.out_at[section], plan.out_width(section) // LANES, plan.counts[section])
        for section in range(3)
    ]
    projected = []
    for section in range(3):
        product = features[section]
        if section < 2:
            copies[section].wait()
            product = contract(product, (l2_ref, l3_ref)[section][...], 1, 0).astype(BF16)
        projected.append(product.reshape(owners, plan.counts[section], width))
    tail = per_owner - sum(plan.counts)
    if tail:
        projected.append(jnp.zeros((owners, tail, width), BF16))
    coarse_ref[...] = jnp.concatenate(projected, axis=1).reshape(owners * per_owner, width)
    copies[2].wait()
    copies[3].wait()

    for turn in range(turns):
        turn_copies[2 * turn].wait()
        turn_copies[2 * turn + 1].wait()
        for owner in range(turn * group, (turn + 1) * group):
            kind = 0 if owner == 0 else 2 if owner == owners - 1 else 1
            start = min(max(owner - 1, 0), owners - 3) * per_owner
            rows = slice(owner * block, (owner + 1) * block)
            joined = straight_ref[rows, :].astype(F32) + contract(
                up_ref[kind], coarse_ref[start : start + reach, :], 1, 0
            )
            gate = 0.5 + 0.5 * jnp.tanh(0.5 * joined)
            hidden = joined * gate
            hidden_ref[rows, :] = hidden.astype(BF16)
            slope = gate + hidden * (1.0 - gate)
            joined_grad_ref[rows, :] = (hidden_grad_ref[rows, :].astype(F32) * slope).astype(BF16)

    for owner in range(owners):
        kind = 0 if owner == 0 else 2 if owner == owners - 1 else 1
        low = min(max(owner * block - 32, 0), total - window)
        strip_grad = contract(down_ref[kind], joined_grad_ref[low : low + window, :], 1, 0)
        for section, ref in enumerate(grad_refs):
            at = plan.starts[section]
            ref[owner] = strip_grad[at : at + plan.counts[section]].astype(BF16)
    strip_grads = [ref[...].reshape(owners * count, width) for ref, count in zip(grad_refs, plan.counts)]
    for section in (1, 2):
        put_pieces(back_ref, plan.back_at[section], strip_grads[section], plan.counts[section])
    put_pieces(back_ref, 0, contract(strip_grads[0], l2_ref[...], 1, 1).astype(BF16), plan.counts[0])
    leaving = [leave(1)]
    two_part_ref[...] = contract(features[0], strip_grads[0], 0, 0)
    three_part_ref[...] = contract(features[1], strip_grads[1], 0, 0)
    for copy in late_copies:
        copy.wait()
    join_part_ref[...] = contract(cot_ref[...], hidden_ref[...], 0, 0)
    one_part_ref[...] = contract(fine_ref[...], joined_grad_ref[...], 0, 0)
    kept, given = stage[2 : 2 + chains], stage[2 + chains :]
    parts = (join_part_ref, two_part_ref, three_part_ref, one_part_ref)

    @pl.when(core == 0)
    def _():
        put_parts(parts, kept, given)

    @pl.when(core != 0)
    def _():
        put_parts(parts, given, kept)

    leaving += [leave(index) for index in range(2, sent)]
    grad_fine_ref[...] = contract(joined_grad_ref[...], l1_ref[...], 1, 1).astype(BF16)
    leaving.append(leave(0))
    for copy in leaving:
        copy.wait()


def finish_kernel(plan, chains, *refs):
    sums, (slices_ref, *pieces), outs = refs[:chains], refs[chains:-5], refs[-5:]
    total = jnp.concatenate([ref[...] for ref in sums])
    join_ref, two_ref, three_ref, one_ref, four_ref = outs
    at = 0
    for ref in (join_ref, two_ref, three_ref, one_ref):
        ref[...] = total[at : at + ref.shape[0]]
        at += ref.shape[0]
    blocks = jnp.concatenate([piece[...] for piece in pieces])
    four_ref[...] = contract(slices_ref[...], blocks, 0, 0)[: four_ref.shape[0]]


def fold_kernel(plan, returned_ref, fold_ref, out_ref):
    arrived = take_pieces(returned_ref, plan.back_at[2], plan.back_width(2) // LANES, plan.counts[2])
    out_ref[...] = contract(fold_ref[...], arrived, 1, 0).astype(BF16)


def section_kernel(plan, *refs):
    sources, outs, held, sem_ref = refs[:6], refs[6:9], refs[9:15], refs[15]
    copies = copies_in(list(zip(sources, held)), sem_ref)
    returned_ref, folds, l3_ref, l4_ref, four_ref = held[0], held[1:3], held[3], held[4], held[5]
    copies[0].wait()
    for section in range(2):
        arrived = take_pieces(
            returned_ref, plan.back_at[section], plan.back_width(section) // LANES, plan.counts[section]
        )
        copies[1 + section].wait()
        folded = contract(folds[section][...], arrived, 1, 0).astype(BF16)
        if section == 1:
            copies[3].wait()
            folded = contract(folded, l3_ref[...], 1, 1).astype(BF16)
        outs[section][...] = folded
    copies[4].wait()
    copies[5].wait()
    outs[2][...] = contract(four_ref[...], l4_ref[...], 1, 1).astype(BF16)


def swap(values, bit):
    owners = lax.axis_size("row")
    return lax.ppermute(values, "row", [(i, i ^ (1 << bit)) for i in range(owners)])


def plus(left, right):
    return (left.astype(F32) + right.astype(F32)).astype(BF16)


class Halving:
    def __init__(self, values, order):
        bits = len(order)
        self.values = values.reshape((2,) * bits + values.shape[1:])
        self.left = sorted(order, reverse=True)
        self.order = list(order)

    def split(self):
        bit = self.order.pop(0)
        axis = self.left.index(bit)
        self.left.pop(axis)
        mine = (lax.axis_index("row") >> bit) & 1
        keep = lax.dynamic_index_in_dim(self.values, mine, axis, keepdims=False)
        give = lax.dynamic_index_in_dim(self.values, 1 - mine, axis, keepdims=False)
        return keep, give, bit

    def step(self, later=None):
        keep, give, bit = self.split()
        if later is not None:
            give, later = lax.optimization_barrier((give, later))
        if self.order:
            self.values = plus(keep, swap(give, bit))
        else:
            self.terms = keep, swap(give, bit)
        return later


def level_swaps(level):
    distances = [0]
    for bit in level:
        distances += [d ^ (1 << bit) for d in distances]
    return distances


def gather_level(stacked, level):
    owners = lax.axis_size("row")
    blocks = {0: stacked}
    for d in level_swaps(level)[1:]:
        if d > 1 and d % 2 == 1:
            blocks[d] = swap(blocks[d - 1], 0)
        else:
            blocks[d] = lax.ppermute(stacked, "row", [(i, i ^ d) for i in range(owners)])
    return list(blocks.values())


def gather_pattern(levels):
    pattern = np.zeros((1,), np.int32)
    for level in levels:
        pattern = np.concatenate([pattern ^ d for d in level_swaps(level)])
    return pattern


def shape_of(*dims, dtype=BF16):
    return jax.ShapeDtypeStruct(dims, dtype)


def body(
    fine_features,
    section_two,
    section_three,
    section_four,
    strip_map,
    lateral_one,
    lateral_two,
    lateral_three,
    lateral_four,
    join_weight,
    cotangent,
):
    owners = lax.axis_size("row")
    bits = owners.bit_length() - 1
    fine_height, strip_width, c1 = fine_features.shape
    width = join_weight.shape[0]
    sections = (section_two, section_three, section_four)
    channels = [s.shape[-1] for s in sections]
    plan = Plan(owners, section_four.shape[0], strip_width, channels, width)
    flats = [s.reshape(-1, s.shape[-1]) for s in sections]
    fine = fine_features.reshape(-1, c1)
    cot = cotangent.reshape(-1, width)
    total = fine.shape[0]
    me = lax.axis_index("row")
    core = (me & 1).astype(jnp.int32).reshape(1)
    up, down = window_matrices(plan)
    exchange = functools.partial(lax.all_to_all, axis_name="row", split_axis=0, concat_axis=0, tiled=True)

    outgoing = pl.pallas_call(
        functools.partial(pack_kernel, plan),
        out_shape=shape_of(owners, plan.sent, LANES),
        in_specs=[SMEM] + [ANY] * 4,
        out_specs=VMEM,
        scratch_shapes=[pltpu.VMEM(x.shape, BF16) for x in (*flats, lateral_four)]
        + [pltpu.VMEM((owners, count, places), BF16) for count, places in zip(plan.counts, plan.coarse)]
        + [pltpu.SemaphoreType.DMA((4,))],
        compiler_params=pltpu.CompilerParams(vmem_limit_bytes=LIMIT),
        name="pack",
    )(strip_map, *flats, lateral_four)
    arrived = exchange(outgoing)
    folds = [fold_matrix(strip_map, plan, section) for section in range(3)]
    arrived, folds = lax.optimization_barrier((arrived, folds))

    half = owners // 2
    heights = [x // owners for x in (width, *channels[:2], c1)]
    chains = CHAINS
    tall = round_up(sum(heights), 8)
    cuts = [round_up(tall * c // chains, 8) for c in range(chains)] + [tall]
    chain_heights = [high - low for low, high in zip(cuts, cuts[1:])]
    early = (lateral_one, fine, join_weight, cot)
    straight, hidden_grad = pl.pallas_call(
        ahead_kernel,
        out_shape=(shape_of(total, width),) * 2,
        in_specs=[ANY] * 4,
        out_specs=(ANY,) * 2,
        scratch_shapes=[pltpu.VMEM(x.shape, BF16) for x in early]
        + [pltpu.VMEM((total, width), BF16)] * 2
        + [pltpu.SemaphoreType.DMA((4,)), pltpu.SemaphoreType.DMA((2,))],
        compiler_params=pltpu.CompilerParams(vmem_limit_bytes=LIMIT),
        cost_estimate=pl.CostEstimate(
            flops=4 * total * width * (width + c1), bytes_accessed=8_000_000, transcendentals=0
        ),
        name="ahead",
    )(*early)
    operands = (
        arrived,
        lateral_two,
        lateral_three,
        up,
        down,
        straight,
        hidden_grad,
        cot,
        fine,
        lateral_one,
    )
    stage = (shape_of(total, c1), shape_of(owners, plan.returned, LANES))
    stage += tuple(shape_of(half, height, width) for height in chain_heights) * 2
    grad_fine, back, *halves = pl.pallas_call(
        functools.partial(strip_kernel, plan, TURNS, chains),
        out_shape=stage,
        in_specs=[SMEM, VMEM] + [ANY] * 9,
        out_specs=(ANY,) * len(stage),
        scratch_shapes=[pltpu.VMEM(x.shape, x.dtype) for x in operands[1:] + stage]
        + [
            pltpu.VMEM((owners * plan.per_owner, width), BF16),
            pltpu.VMEM((total, width), BF16),
            pltpu.VMEM((total, width), BF16),
        ]
        + [pltpu.VMEM((owners, count, width), BF16) for count in plan.counts]
        + [pltpu.VMEM((x, width), F32) for x in (width, *channels[:2], c1)]
        + [
            pltpu.SemaphoreType.DMA((len(stage),)),
            pltpu.SemaphoreType.DMA((7,)),
            pltpu.SemaphoreType.DMA((2, TURNS)),
        ],
        compiler_params=pltpu.CompilerParams(vmem_limit_bytes=STRIP),
        cost_estimate=pl.CostEstimate(
            flops=4_000_000_000, bytes_accessed=16_000_000, transcendentals=total * width
        ),
        name="strip_work",
    )(core, *operands)

    levels = tuple(range(bits - 2, bits)), tuple(range(bits - 2))
    slices = jnp.take(arrived[:, plan.slice_at :], me ^ gather_pattern(levels), axis=0)
    grad_fine = jnp.transpose(grad_fine.reshape(fine_features.shape), (1, 2, 0))
    rest = [
        Halving(plus(keep, swap(give, 0)), range(1, bits))
        for keep, give in zip(halves[:chains], halves[chains:])
    ]
    halved = [chain.split() for chain in rest]
    halved = [(keep, swap(give, bit)) for keep, give, bit in halved]
    returned = exchange(back)
    returned, grad_fine, slices = lax.optimization_barrier((returned, grad_fine, slices))

    folded_four = pl.pallas_call(
        functools.partial(fold_kernel, plan),
        out_shape=shape_of(plan.coarse[2], width),
        in_specs=[VMEM] * 2,
        out_specs=VMEM,
        compiler_params=pltpu.CompilerParams(vmem_limit_bytes=8 * MEBI),
        name="fold_four",
    )(returned, folds[2])
    *halved, folded_four = lax.optimization_barrier((*halved, folded_four))
    for chain, (keep, received) in zip(rest, halved):
        chain.values = plus(keep, received)
    operands = (returned, *folds[:2], lateral_three, lateral_four, folded_four)
    grads = pl.pallas_call(
        functools.partial(section_kernel, plan),
        out_shape=tuple(shape_of(*f.shape) for f in flats),
        in_specs=[ANY] * 6,
        out_specs=(VMEM,) * 3,
        scratch_shapes=[pltpu.VMEM(x.shape, BF16) for x in operands] + [pltpu.SemaphoreType.DMA((6,))],
        compiler_params=pltpu.CompilerParams(vmem_limit_bytes=SMALL),
        cost_estimate=pl.CostEstimate(flops=500_000_000, bytes_accessed=6_000_000, transcendentals=0),
        name="section_grads",
    )(*operands)

    gathered = folded_four[None]
    for turn in range(bits - 2):
        if turn == 0:
            gathered = jnp.concatenate(gather_level(gathered, levels[0]))
            for chain in rest:
                chain.step()
        else:
            for chain in rest:
                gathered = chain.step(gathered)
        if turn < bits - 3:
            *values, grads, gathered = lax.optimization_barrier(
                (*[chain.values for chain in rest], grads, gathered)
            )
            for chain, value in zip(rest, values):
                chain.values = value
    gathered = gather_level(gathered, levels[1])

    sums = [keep.astype(F32) + received.astype(F32) for keep, received in (chain.terms for chain in rest)]
    *sums, gathered = lax.optimization_barrier((*sums, gathered))
    operands = tuple(sums)
    operands += (slices.reshape(-1, LANES), *[g.reshape(-1, width) for g in gathered])
    results = pl.pallas_call(
        functools.partial(finish_kernel, plan, chains),
        out_shape=(
            *[shape_of(height, width, dtype=F32) for height in heights],
            shape_of(plan.slice_width, width, dtype=F32),
        ),
        in_specs=[VMEM] * len(operands),
        out_specs=(VMEM,) * 5,
        compiler_params=pltpu.CompilerParams(vmem_limit_bytes=16 * MEBI),
        name="finish",
    )(*operands)
    join_grad, two_grad, three_grad, one_grad, four_grad = results
    return (
        jnp.transpose(grad_fine, (2, 0, 1)),
        *[g.reshape(s.shape) for g, s in zip(grads, sections)],
        join_grad.T,
        one_grad,
        two_grad,
        three_grad,
        four_grad,
    )


def solution(mesh):
    fine_spec = P(None, ("group", "row"), None)
    coarse_spec = P("row", "group", None)
    weight_spec = P(("group", "row"), None)
    return jax.shard_map(
        body,
        mesh=mesh,
        in_specs=(fine_spec,) + (coarse_spec,) * 3 + (P("group"),) + (P(),) * 5 + (fine_spec,),
        out_specs=(fine_spec,) + (coarse_spec,) * 3 + (P("group", "row"),) + (weight_spec,) * 4,
        check_vma=False,
    )
```

```python
import functools

import jax
import jax.numpy as jnp
import numpy as np
from jax import lax
from jax.experimental import pallas as pl
from jax.experimental.pallas import tpu as pltpu
from jax.sharding import PartitionSpec as P

F32 = jnp.float32
BF16 = jnp.bfloat16
FACTORS = (2, 4, 8)
LANES = 128
VMEM = pl.BlockSpec(memory_space=pltpu.VMEM)
SMEM = pl.BlockSpec(memory_space=pltpu.SMEM)
ANY = pl.BlockSpec(memory_space=pl.ANY)
MEBI = 1024 * 1024
LIMIT = 62 * MEBI
SMALL = 62 * MEBI
STRIP = 58 * MEBI
TURNS = 4
CHAINS = 1


def round_up(value, multiple):
    return -(-value // multiple) * multiple


class Plan:
    def __init__(self, owners, depth, strip_width, channels, width):
        self.owners, self.depth, self.strip_width = owners, depth, strip_width
        self.channels, self.width = channels, width
        self.rows = [depth * 8 // k for k in FACTORS]
        self.columns = [strip_width // k for k in FACTORS]
        self.coarse = [r * c * owners for r, c in zip(self.rows, self.columns)]
        self.entries, self.counts, self.starts = [], [], []
        at = 0
        for rows, columns in zip(self.rows, self.columns):
            entries = [(r, c) for r in range(rows) for c in range(columns + 2)]
            entries += [None] * (-len(entries) % 8)
            self.entries.append(entries)
            self.counts.append(len(entries))
            self.starts.append(at)
            at += len(entries)
        self.per_owner = round_up(at, 16)
        self.out_at, self.back_at = [], []
        self.sent = self.returned = 0
        for section in range(3):
            self.out_at.append(self.sent)
            self.sent += self.counts[section] * (self.out_width(section) // LANES)
        for section in range(3):
            self.back_at.append(self.returned)
            self.returned += self.counts[section] * (self.back_width(section) // LANES)
        self.slice_at = self.sent
        self.slice_width = channels[2] // owners
        spare = LANES - self.slice_width
        cut = self.slice_width // spare if spare and self.slice_width % spare == 0 else 0
        folded = self.coarse[2] // (cut + 1) if cut and self.coarse[2] % (8 * (cut + 1)) == 0 else 0
        self.folded, self.cut, self.spare = folded, cut if folded else 0, spare
        self.sent += self.coarse[2] - folded

    def out_width(self, section):
        return self.channels[section] if section < 2 else self.width

    def back_width(self, section):
        return self.channels[0] if section == 0 else self.width


def axis_weights(fine_count, factor):
    matrix = np.zeros((fine_count, fine_count // factor + 2), np.float32)
    for fine in range(fine_count):
        base, phase = divmod(fine, factor)
        offset = (phase + 0.5) / factor - 0.5
        if offset < 0:
            matrix[fine, base] += -offset
            matrix[fine, base + 1] += 1.0 + offset
        else:
            matrix[fine, base + 1] += 1.0 - offset
            matrix[fine, base + 2] += offset
    return matrix


def clamp_rows(matrix):
    folded = matrix[:, 1:-1].copy()
    folded[:, 0] += matrix[:, 0]
    folded[:, -1] += matrix[:, -1]
    return folded


def window_matrices(plan):
    owners, strip_width = plan.owners, plan.strip_width
    block_rows = plan.depth * 8
    fine_rows = owners * block_rows
    whole = np.zeros((fine_rows, strip_width, owners, plan.per_owner), np.float32)
    row_mats = [clamp_rows(axis_weights(fine_rows, k)) for k in FACTORS]
    col_mats = [axis_weights(strip_width, k) for k in FACTORS]
    for owner in range(owners):
        for section in range(3):
            for index, entry in enumerate(plan.entries[section]):
                if entry is not None:
                    at = owner * plan.rows[section] + entry[0]
                    whole[:, :, owner, plan.starts[section] + index] = np.outer(
                        row_mats[section][:, at], col_mats[section][:, entry[1]]
                    )
    up, down = [], []
    for owner in (0, 1, owners - 1):
        start = min(max(owner - 1, 0), owners - 3)
        rows = slice(owner * block_rows, (owner + 1) * block_rows)
        up.append(
            whole[rows, :, start : start + 3].reshape(block_rows * strip_width, 3 * plan.per_owner)
        )
        window = block_rows + 8
        low = min(max(owner * block_rows - 4, 0), fine_rows - window)
        piece = whole[low : low + window, :, owner]
        down.append(piece.reshape(window * strip_width, plan.per_owner).T)
    return np.stack(up).astype(BF16), np.stack(down).astype(BF16)


def entry_tables(plan, section):
    entries, columns = plan.entries[section], plan.columns[section]
    start = [-(1 << 20) if e is None else e[0] * columns * plan.owners for e in entries]
    offset = [0 if e is None else e[1] - 1 for e in entries]
    return np.array(start, np.int32), np.array(offset, np.int32)


def fold_matrix(strip_map, plan, section):
    start, offset = entry_tables(plan, section)
    columns = plan.columns[section]
    column = jnp.clip(strip_map[:, None] * columns + offset, 0, plan.owners * columns - 1)
    target = (column + start).reshape(-1)
    places = np.arange(plan.coarse[section], dtype=np.int32)
    return (places[:, None] == target[None]).astype(BF16)


def contract(left, right, left_dim, right_dim):
    return lax.dot_general(
        left, right, (((left_dim,), (right_dim,)), ((), ())), preferred_element_type=F32
    )


def put_pieces(ref, at, values, count):
    owners = ref.shape[0]
    for piece in range(values.shape[1] // LANES):
        part = values[:, piece * LANES : (piece + 1) * LANES]
        ref[:, at + piece * count : at + (piece + 1) * count, :] = part.reshape(owners, count, LANES)


def take_pieces(ref, at, pieces, count):
    owners = ref.shape[0]
    return jnp.concatenate(
        [
            ref[:, at + p * count : at + (p + 1) * count, :].reshape(owners * count, LANES)
            for p in range(pieces)
        ],
        axis=1,
    )


def copies_in(pairs, sem_ref):
    copies = [pltpu.make_async_copy(src, dst, sem_ref.at[i]) for i, (src, dst) in enumerate(pairs)]
    for copy in copies:
        copy.start()
    return copies


def entry_vectors(plan, section, shape):
    entry = lax.broadcasted_iota(jnp.int32, shape, 0)
    columns = plan.columns[section]
    span = columns + 2
    scale = -(-65536 // span)
    assert all((q * scale) >> 16 == q // span for q in range(shape[0]))
    row = (entry * scale) >> 16
    start = jnp.where(row < plan.rows[section], row * (columns * plan.owners), -(1 << 20))
    return start, entry - row * span - 1


def pack_kernel(plan, map_ref, *refs):
    sources, out_ref = refs[:4], refs[4]
    held, picks, sem_ref = refs[5:9], refs[9:12], refs[12]
    copies = copies_in(list(zip(sources, held)), sem_ref)
    four_ref, l4_ref = held[2:]
    for section in range(3):
        columns, count, places = plan.columns[section], plan.counts[section], plan.coarse[section]
        start, offset = entry_vectors(plan, section, (count, min(LANES, places)))
        lane = lax.broadcasted_iota(jnp.int32, start.shape, 1) - start
        for device in range(plan.owners):
            column = jnp.clip(map_ref[device] * columns + offset, 0, plan.owners * columns - 1)
            ahead = lane - column
            for at in range(0, places, LANES):
                picks[section][device, :, at : at + LANES] = jnp.where(ahead == -at, 1.0, 0.0).astype(BF16)
    for section in range(3):
        count = plan.counts[section]
        pick = picks[section][...].reshape(plan.owners * count, plan.coarse[section])
        copies[section].wait()
        values = held[section][...]
        if section == 2:
            copies[3].wait()
            values = contract(values, l4_ref[...], 1, 0).astype(BF16)
        put_pieces(out_ref, plan.out_at[section], contract(pick, values, 1, 0).astype(BF16), count)
    count = plan.coarse[2] - plan.folded
    fill = jnp.zeros((count, plan.spare), BF16)
    for owner in range(plan.owners):
        part = four_ref[:, owner * plan.slice_width : (owner + 1) * plan.slice_width]
        if plan.folded:
            last = part[count:]
            fill = jnp.concatenate(
                [last[:, piece * plan.spare : (piece + 1) * plan.spare] for piece in range(plan.cut)]
            )
        out_ref[owner, plan.slice_at :, :] = jnp.concatenate([part[:count], fill], axis=1)


def put_parts(part_refs, even_refs, odd_refs):
    owners = 2 * even_refs[0].shape[0]
    for owner in range(owners):
        refs = (even_refs, odd_refs)[owner % 2]
        index, at = 0, 0
        for part_ref in part_refs:
            height = part_ref.shape[0] // owners
            done = 0
            while done < height:
                if at == refs[index].shape[1]:
                    index, at = index + 1, 0
                count = min(height - done, refs[index].shape[1] - at)
                first = owner * height + done
                refs[index][owner // 2, at : at + count, :] = part_ref[first : first + count, :].astype(BF16)
                done += count
                at += count
        if at < refs[index].shape[1]:
            fill = jnp.zeros((refs[index].shape[1] - at, refs[index].shape[2]), BF16)
            refs[index][owner // 2, at:, :] = fill


def ahead_kernel(*refs):
    sources, outs = refs[:4], refs[4:6]
    held, stage, in_sem, out_sem = refs[6:10], refs[10:12], refs[12], refs[13]
    l1_ref, fine_ref, join_ref, cot_ref = held
    copies = copies_in(list(zip(sources, held)), in_sem)
    copies[0].wait()
    copies[1].wait()
    stage[0][...] = contract(fine_ref[...], l1_ref[...], 1, 0).astype(BF16)
    first = pltpu.make_async_copy(stage[0], outs[0], out_sem.at[0])
    first.start()
    copies[2].wait()
    copies[3].wait()
    stage[1][...] = contract(cot_ref[...], join_ref[...], 1, 1).astype(BF16)
    second = pltpu.make_async_copy(stage[1], outs[1], out_sem.at[1])
    second.start()
    first.wait()
    second.wait()


def take_features(plan, arrived_ref, section):
    return take_pieces(
        arrived_ref, plan.out_at[section], plan.out_width(section) // LANES, plan.counts[section]
    )


def strip_kernel(plan, turns, chains, core_ref, *refs):
    sent = 2 + 2 * chains
    arrived_ref, sources, outs = refs[0], refs[1:10], refs[10 : 10 + sent]
    held, stage, refs = refs[10 + sent : 19 + sent], refs[19 + sent : 19 + 2 * sent], refs[19 + 2 * sent :]
    l2_ref, l3_ref, up_ref, down_ref, straight_ref, hidden_grad_ref, cot_ref, fine_ref, l1_ref = held
    grad_fine_ref, back_ref = stage[:2]
    coarse_ref, hidden_ref, joined_grad_ref = refs[:3]
    grad_refs = refs[3:6]
    join_part_ref, two_part_ref, three_part_ref, one_part_ref, out_sem, in_sem, turn_sem = refs[6:]
    owners, per_owner, width = plan.owners, plan.per_owner, plan.width
    core = core_ref[0]
    block = up_ref.shape[1]
    reach = up_ref.shape[2]
    window = down_ref.shape[2]
    total = cot_ref.shape[0]
    group = owners // turns
    copies = copies_in(list(zip(sources[:4], held[:4])), in_sem)
    turn_copies = []
    for turn in range(turns):
        many = pl.ds(turn * group * block, group * block)
        for which in (0, 1):
            copy = pltpu.make_async_copy(
                sources[4 + which].at[many], held[4 + which].at[many], turn_sem.at[which, turn]
            )
            copy.start()
            turn_copies.append(copy)
    late_copies = []
    for index in (6, 7, 8):
        copy = pltpu.make_async_copy(sources[index], held[index], in_sem.at[index - 2])
        copy.start()
        late_copies.append(copy)

    def leave(index):
        copy = pltpu.make_async_copy(stage[index], outs[index], out_sem.at[index])
        copy.start()
        return copy

    features = [
        take_pieces(arrived_ref, plan.out_at[section], plan.out_width(section) // LANES, plan.counts[section])
        for section in range(3)
    ]
    projected = []
    for section in range(3):
        product = features[section]
        if section < 2:
            copies[section].wait()
            product = contract(product, (l2_ref, l3_ref)[section][...], 1, 0).astype(BF16)
        projected.append(product.reshape(owners, plan.counts[section], width))
    tail = per_owner - sum(plan.counts)
    if tail:
        projected.append(jnp.zeros((owners, tail, width), BF16))
    coarse_ref[...] = jnp.concatenate(projected, axis=1).reshape(owners * per_owner, width)
    copies[2].wait()
    copies[3].wait()

    for turn in range(turns):
        turn_copies[2 * turn].wait()
        turn_copies[2 * turn + 1].wait()
        for owner in range(turn * group, (turn + 1) * group):
            kind = 0 if owner == 0 else 2 if owner == owners - 1 else 1
            start = min(max(owner - 1, 0), owners - 3) * per_owner
            rows = slice(owner * block, (owner + 1) * block)
            joined = straight_ref[rows, :].astype(F32) + contract(
                up_ref[kind], coarse_ref[start : start + reach, :], 1, 0
            )
            gate = 0.5 + 0.5 * jnp.tanh(0.5 * joined)
            hidden = joined * gate
            hidden_ref[rows, :] = hidden.astype(BF16)
            slope = gate + hidden * (1.0 - gate)
            joined_grad_ref[rows, :] = (hidden_grad_ref[rows, :].astype(F32) * slope).astype(BF16)

    for owner in range(owners):
        kind = 0 if owner == 0 else 2 if owner == owners - 1 else 1
        low = min(max(owner * block - 32, 0), total - window)
        strip_grad = contract(down_ref[kind], joined_grad_ref[low : low + window, :], 1, 0)
        for section, ref in enumerate(grad_refs):
            at = plan.starts[section]
            ref[owner] = strip_grad[at : at + plan.counts[section]].astype(BF16)
    strip_grads = [ref[...].reshape(owners * count, width) for ref, count in zip(grad_refs, plan.counts)]
    for section in (1, 2):
        put_pieces(back_ref, plan.back_at[section], strip_grads[section], plan.counts[section])
    put_pieces(back_ref, 0, contract(strip_grads[0], l2_ref[...], 1, 1).astype(BF16), plan.counts[0])
    leaving = [leave(1)]
    two_part_ref[...] = contract(features[0], strip_grads[0], 0, 0)
    three_part_ref[...] = contract(features[1], strip_grads[1], 0, 0)
    for copy in late_copies:
        copy.wait()
    join_part_ref[...] = contract(cot_ref[...], hidden_ref[...], 0, 0)
    one_part_ref[...] = contract(fine_ref[...], joined_grad_ref[...], 0, 0)
    kept, given = stage[2 : 2 + chains], stage[2 + chains :]
    parts = (join_part_ref, two_part_ref, three_part_ref, one_part_ref)

    @pl.when(core == 0)
    def _():
        put_parts(parts, kept, given)

    @pl.when(core != 0)
    def _():
        put_parts(parts, given, kept)

    leaving += [leave(index) for index in range(2, sent)]
    grad_fine_ref[...] = contract(joined_grad_ref[...], l1_ref[...], 1, 1).astype(BF16)
    leaving.append(leave(0))
    for copy in leaving:
        copy.wait()


def finish_kernel(plan, chains, *refs):
    sums, (slices_ref, *pieces), outs = refs[:chains], refs[chains:-5], refs[-5:]
    total = jnp.concatenate([ref[...] for ref in sums])
    join_ref, two_ref, three_ref, one_ref, four_ref = outs
    at = 0
    for ref in (join_ref, two_ref, three_ref, one_ref):
        ref[...] = total[at : at + ref.shape[0]]
        at += ref.shape[0]
    blocks = jnp.concatenate([piece[...] for piece in pieces])
    four_ref[...] = contract(slices_ref[...], blocks, 0, 0)[: four_ref.shape[0]]


def fold_kernel(plan, returned_ref, fold_ref, out_ref):
    arrived = take_pieces(returned_ref, plan.back_at[2], plan.back_width(2) // LANES, plan.counts[2])
    out_ref[...] = contract(fold_ref[...], arrived, 1, 0).astype(BF16)


def section_kernel(plan, *refs):
    sources, outs, held, sem_ref = refs[:6], refs[6:9], refs[9:15], refs[15]
    copies = copies_in(list(zip(sources, held)), sem_ref)
    returned_ref, folds, l3_ref, l4_ref, four_ref = held[0], held[1:3], held[3], held[4], held[5]
    copies[0].wait()
    for section in range(2):
        arrived = take_pieces(
            returned_ref, plan.back_at[section], plan.back_width(section) // LANES, plan.counts[section]
        )
        copies[1 + section].wait()
        folded = contract(folds[section][...], arrived, 1, 0).astype(BF16)
        if section == 1:
            copies[3].wait()
            folded = contract(folded, l3_ref[...], 1, 1).astype(BF16)
        outs[section][...] = folded
    copies[4].wait()
    copies[5].wait()
    outs[2][...] = contract(four_ref[...], l4_ref[...], 1, 1).astype(BF16)


def swap(values, bit):
    owners = lax.axis_size("row")
    return lax.ppermute(values, "row", [(i, i ^ (1 << bit)) for i in range(owners)])


def plus(left, right):
    return (left.astype(F32) + right.astype(F32)).astype(BF16)


class Halving:
    def __init__(self, values, order):
        bits = len(order)
        self.values = values.reshape((2,) * bits + values.shape[1:])
        self.left = sorted(order, reverse=True)
        self.order = list(order)

    def split(self):
        bit = self.order.pop(0)
        axis = self.left.index(bit)
        self.left.pop(axis)
        mine = (lax.axis_index("row") >> bit) & 1
        keep = lax.dynamic_index_in_dim(self.values, mine, axis, keepdims=False)
        give = lax.dynamic_index_in_dim(self.values, 1 - mine, axis, keepdims=False)
        return keep, give, bit

    def step(self, later=None):
        keep, give, bit = self.split()
        if later is not None:
            give, later = lax.optimization_barrier((give, later))
        if self.order:
            self.values = plus(keep, swap(give, bit))
        else:
            self.terms = keep, swap(give, bit)
        return later


def level_swaps(level):
    distances = [0]
    for bit in level:
        distances += [d ^ (1 << bit) for d in distances]
    return distances


def gather_level(stacked, level):
    owners = lax.axis_size("row")
    blocks = {0: stacked}
    for d in level_swaps(level)[1:]:
        if d > 1 and d % 2 == 1:
            blocks[d] = swap(blocks[d - 1], 0)
        else:
            blocks[d] = lax.ppermute(stacked, "row", [(i, i ^ d) for i in range(owners)])
    return list(blocks.values())


def gather_pattern(levels):
    pattern = np.zeros((1,), np.int32)
    for level in levels:
        pattern = np.concatenate([pattern ^ d for d in level_swaps(level)])
    return pattern


def unfold_slices(plan, slices):
    parts = [slices[..., : plan.slice_width]]
    if plan.folded:
        spare = slices[..., plan.slice_width :].reshape(plan.owners, plan.cut, plan.folded, plan.spare)
        parts.append(jnp.moveaxis(spare, 1, 2).reshape(plan.owners, plan.folded, plan.slice_width))
    return jnp.concatenate(parts, axis=1).reshape(-1, plan.slice_width)


def shape_of(*dims, dtype=BF16):
    return jax.ShapeDtypeStruct(dims, dtype)


def body(
    fine_features,
    section_two,
    section_three,
    section_four,
    strip_map,
    lateral_one,
    lateral_two,
    lateral_three,
    lateral_four,
    join_weight,
    cotangent,
):
    owners = lax.axis_size("row")
    bits = owners.bit_length() - 1
    fine_height, strip_width, c1 = fine_features.shape
    width = join_weight.shape[0]
    sections = (section_two, section_three, section_four)
    channels = [s.shape[-1] for s in sections]
    plan = Plan(owners, section_four.shape[0], strip_width, channels, width)
    flats = [s.reshape(-1, s.shape[-1]) for s in sections]
    fine = fine_features.reshape(-1, c1)
    cot = cotangent.reshape(-1, width)
    total = fine.shape[0]
    me = lax.axis_index("row")
    core = (me & 1).astype(jnp.int32).reshape(1)
    up, down = window_matrices(plan)
    exchange = functools.partial(lax.all_to_all, axis_name="row", split_axis=0, concat_axis=0, tiled=True)

    outgoing = pl.pallas_call(
        functools.partial(pack_kernel, plan),
        out_shape=shape_of(owners, plan.sent, LANES),
        in_specs=[SMEM] + [ANY] * 4,
        out_specs=VMEM,
        scratch_shapes=[pltpu.VMEM(x.shape, BF16) for x in (*flats, lateral_four)]
        + [pltpu.VMEM((owners, count, places), BF16) for count, places in zip(plan.counts, plan.coarse)]
        + [pltpu.SemaphoreType.DMA((4,))],
        compiler_params=pltpu.CompilerParams(vmem_limit_bytes=LIMIT),
        name="pack",
    )(strip_map, *flats, lateral_four)
    arrived = exchange(outgoing)
    folds = [fold_matrix(strip_map, plan, section) for section in range(3)]
    arrived, folds = lax.optimization_barrier((arrived, folds))

    half = owners // 2
    heights = [x // owners for x in (width, *channels[:2], c1)]
    chains = CHAINS
    tall = round_up(sum(heights), 8)
    cuts = [round_up(tall * c // chains, 8) for c in range(chains)] + [tall]
    chain_heights = [high - low for low, high in zip(cuts, cuts[1:])]
    early = (lateral_one, fine, join_weight, cot)
    straight, hidden_grad = pl.pallas_call(
        ahead_kernel,
        out_shape=(shape_of(total, width),) * 2,
        in_specs=[ANY] * 4,
        out_specs=(ANY,) * 2,
        scratch_shapes=[pltpu.VMEM(x.shape, BF16) for x in early]
        + [pltpu.VMEM((total, width), BF16)] * 2
        + [pltpu.SemaphoreType.DMA((4,)), pltpu.SemaphoreType.DMA((2,))],
        compiler_params=pltpu.CompilerParams(vmem_limit_bytes=LIMIT),
        cost_estimate=pl.CostEstimate(
            flops=4 * total * width * (width + c1), bytes_accessed=8_000_000, transcendentals=0
        ),
        name="ahead",
    )(*early)
    operands = (
        arrived,
        lateral_two,
        lateral_three,
        up,
        down,
        straight,
        hidden_grad,
        cot,
        fine,
        lateral_one,
    )
    stage = (shape_of(total, c1), shape_of(owners, plan.returned, LANES))
    stage += tuple(shape_of(half, height, width) for height in chain_heights) * 2
    grad_fine, back, *halves = pl.pallas_call(
        functools.partial(strip_kernel, plan, TURNS, chains),
        out_shape=stage,
        in_specs=[SMEM, VMEM] + [ANY] * 9,
        out_specs=(ANY,) * len(stage),
        scratch_shapes=[pltpu.VMEM(x.shape, x.dtype) for x in operands[1:] + stage]
        + [
            pltpu.VMEM((owners * plan.per_owner, width), BF16),
            pltpu.VMEM((total, width), BF16),
            pltpu.VMEM((total, width), BF16),
        ]
        + [pltpu.VMEM((owners, count, width), BF16) for count in plan.counts]
        + [pltpu.VMEM((x, width), F32) for x in (width, *channels[:2], c1)]
        + [
            pltpu.SemaphoreType.DMA((len(stage),)),
            pltpu.SemaphoreType.DMA((7,)),
            pltpu.SemaphoreType.DMA((2, TURNS)),
        ],
        compiler_params=pltpu.CompilerParams(vmem_limit_bytes=STRIP),
        cost_estimate=pl.CostEstimate(
            flops=4_000_000_000, bytes_accessed=16_000_000, transcendentals=total * width
        ),
        name="strip_work",
    )(core, *operands)

    levels = tuple(range(bits - 2, bits)), tuple(range(bits - 2))
    slices = unfold_slices(plan, jnp.take(arrived[:, plan.slice_at :], me ^ gather_pattern(levels), axis=0))
    grad_fine = jnp.transpose(grad_fine.reshape(fine_features.shape), (1, 2, 0))
    rest = [
        Halving(plus(keep, swap(give, 0)), range(1, bits))
        for keep, give in zip(halves[:chains], halves[chains:])
    ]
    halved = [chain.split() for chain in rest]
    halved = [(keep, swap(give, bit)) for keep, give, bit in halved]
    returned = exchange(back)
    returned, grad_fine, slices = lax.optimization_barrier((returned, grad_fine, slices))

    folded_four = pl.pallas_call(
        functools.partial(fold_kernel, plan),
        out_shape=shape_of(plan.coarse[2], width),
        in_specs=[VMEM] * 2,
        out_specs=VMEM,
        compiler_params=pltpu.CompilerParams(vmem_limit_bytes=8 * MEBI),
        name="fold_four",
    )(returned, folds[2])
    *halved, folded_four = lax.optimization_barrier((*halved, folded_four))
    for chain, (keep, received) in zip(rest, halved):
        chain.values = plus(keep, received)
    operands = (returned, *folds[:2], lateral_three, lateral_four, folded_four)
    grads = pl.pallas_call(
        functools.partial(section_kernel, plan),
        out_shape=tuple(shape_of(*f.shape) for f in flats),
        in_specs=[ANY] * 6,
        out_specs=(VMEM,) * 3,
        scratch_shapes=[pltpu.VMEM(x.shape, BF16) for x in operands] + [pltpu.SemaphoreType.DMA((6,))],
        compiler_params=pltpu.CompilerParams(vmem_limit_bytes=SMALL),
        cost_estimate=pl.CostEstimate(flops=500_000_000, bytes_accessed=6_000_000, transcendentals=0),
        name="section_grads",
    )(*operands)

    gathered = folded_four[None]
    for turn in range(bits - 2):
        if turn == 0:
            gathered = jnp.concatenate(gather_level(gathered, levels[0]))
            for chain in rest:
                chain.step()
        else:
            for chain in rest:
                gathered = chain.step(gathered)
        if turn < bits - 3:
            *values, grads, gathered = lax.optimization_barrier(
                (*[chain.values for chain in rest], grads, gathered)
            )
            for chain, value in zip(rest, values):
                chain.values = value
    gathered = gather_level(gathered, levels[1])

    sums = [keep.astype(F32) + received.astype(F32) for keep, received in (chain.terms for chain in rest)]
    *sums, gathered = lax.optimization_barrier((*sums, gathered))
    operands = tuple(sums)
    operands += (slices, *[g.reshape(-1, width) for g in gathered])
    results = pl.pallas_call(
        functools.partial(finish_kernel, plan, chains),
        out_shape=(
            *[shape_of(height, width, dtype=F32) for height in heights],
            shape_of(plan.slice_width, width, dtype=F32),
        ),
        in_specs=[VMEM] * len(operands),
        out_specs=(VMEM,) * 5,
        compiler_params=pltpu.CompilerParams(vmem_limit_bytes=16 * MEBI),
        name="finish",
    )(*operands)
    join_grad, two_grad, three_grad, one_grad, four_grad = results
    return (
        jnp.transpose(grad_fine, (2, 0, 1)),
        *[g.reshape(s.shape) for g, s in zip(grads, sections)],
        join_grad.T,
        one_grad,
        two_grad,
        three_grad,
        four_grad,
    )


def solution(mesh):
    fine_spec = P(None, ("group", "row"), None)
    coarse_spec = P("row", "group", None)
    weight_spec = P(("group", "row"), None)
    return jax.shard_map(
        body,
        mesh=mesh,
        in_specs=(fine_spec,) + (coarse_spec,) * 3 + (P("group"),) + (P(),) * 5 + (fine_spec,),
        out_specs=(fine_spec,) + (coarse_spec,) * 3 + (P("group", "row"),) + (weight_spec,) * 4,
        check_vma=False,
    )
```
